32 devices in a mesh: segment: 2 (over y), ulysses: 8 (over z, x), rep: 2 (over core).
Axes of the slice: x: 2, y: 2, z: 4, core: 2. Of those that a mesh axis runs over, the one named last changes fastest.
Arguments:
- hidden_in: bfloat16 [512, 3072], P('rep'), parts along dimension 0, may hold values from -6 to 6
- assign: int32 [256], replicated, may hold values from 0 to 255, each once
- order: int32 [4], replicated, may hold values from 0 to 3, each once
- w_qkv: bfloat16 [2, 3072, 3, 1024], P('segment', None, None, 'ulysses'), may hold values from -0.109375 to 0.109375
- w_out: bfloat16 [2, 1024, 3072], P('segment', 'ulysses'), may hold values from -0.1875 to 0.1875
- mod_shift: float32 [2, 3072], P('segment'), may hold values from -3 to 3
- mod_scale: float32 [2, 3072], P('segment'), may hold values from -3 to 3
- mod_gate: float32 [2, 3072], P('segment'), may hold values from 1 to 3
- q_gain: float32 [2, 128], P('segment'), may hold values from 0.5 to 2
- k_gain: float32 [2, 128], P('segment'), may hold values from 0.5 to 2
- stale_keys: bfloat16 [2, 512, 1024], P('segment', 'rep', 'ulysses'), parts along dimension 1, may hold values from -6 to 6
- stale_values: bfloat16 [2, 512, 1024], P('segment', 'rep', 'ulysses'), parts along dimension 1, may hold values from -6 to 6
Outputs:
- block_out: bfloat16 [2, 8, 64, 3072], P('segment', 'rep', 'ulysses'), parts along dimension 1
- new_keys: bfloat16 [2, 512, 1024], P('segment', 'rep', 'ulysses'), parts along dimension 1
- new_values: bfloat16 [2, 512, 1024], P('segment', 'rep', 'ulysses'), parts along dimension 1
The draws below stay inside these ranges and needn't reach their ends.
There are 2 independent parts, one for each index of `rep`. The reference program is written for one: setup_inputs(seed, part) draws one part's arguments, and reference() takes and returns one part's arrays. A program takes and returns all parts, laid end to end along the dimension named above; an argument that names none is the same for every part. Nothing has to cross between parts.
Inputs may be any that keep to these rules, and one draw needn't show every extreme that they name: `assign`: a permutation. `order`: a permutation.
All inputs are finite; a program needn't handle non-finite values.
Results may differ from the reference program's by a relative error of at most 0.03.
Values may be sent and summed in bfloat16 or wider, within the bound.
A program may use at most 64 MiB of HBM per device.

```python
import math
import jax
import jax.numpy as jnp
from jax import lax

D = 3072
HD = 128
PATCHES = 4
HEADS = 8
TOKENS = 256
LAYERS = 2


def block_scale(key, dims, split, least, high):
    level, own = 1.0, jax.random.fold_in(key, 6)
    for dim, blocks in split:
        draws = jnp.exp(jax.random.uniform(jax.random.fold_in(own, dim), (blocks,), jnp.float32, least / len(split), high / len(split)))
        level = level * jnp.repeat(draws, dims[dim] // blocks).reshape([-1 if axis == dim else 1 for axis in range(len(dims))])
    return level


def centred(key, dims, scale, bound, shards=(), kind=jnp.bfloat16):
    result = jax.random.normal(key, dims, jnp.float32) * scale
    if len(shards) > 0:
        result = block_scale(key, dims, shards, -0.22, 0.18) * result
    return jnp.clip(result, min=-bound, max=bound).astype(kind)


def setup_inputs(seed: int = 0, part: int = 0) -> dict:
    splits = jax.random.split(jax.random.key(seed), 13)
    part_keys = jax.random.split(jax.random.fold_in(splits[12], part), 13)
    return {
        "hidden_in": centred(part_keys[0], (TOKENS, D), 1.0, 6.0),
        "assign": jax.random.permutation(splits[1], TOKENS).astype(jnp.int32),
        "order": jax.random.permutation(splits[2], PATCHES).astype(jnp.int32),
        "w_qkv": centred(splits[3], (LAYERS, D, 3, HEADS * HD), D ** -0.5, 0.109375, ((0, 2), (3, 8))),
        "w_out": centred(splits[4], (LAYERS, HEADS * HD, D), (HEADS * HD) ** -0.5, 0.1875, ((0, 2), (1, 8))),
        "mod_shift": centred(splits[5], (LAYERS, D), 0.5, 3.0, ((0, 2),), jnp.float32),
        "mod_scale": centred(splits[6], (LAYERS, D), 0.5, 3.0, ((0, 2),), jnp.float32),
        "mod_gate": jnp.clip(1.0 + 2.0 * jax.random.uniform(splits[7], (LAYERS, D), jnp.float32) ** block_scale(splits[7], (LAYERS, D), ((0, 2),), -0.2, 0.2), 1.0, 3.0),
        "q_gain": jnp.clip(jnp.exp(math.log(2.0) - 1.3862944 * jax.random.uniform(splits[8], (LAYERS, HD), jnp.float32) ** block_scale(splits[8], (LAYERS, HD), ((0, 2),), -0.2, 0.2)), 0.5, 2.0),
        "k_gain": jnp.clip(jnp.exp(math.log(2.0) - 1.3862944 * jax.random.uniform(splits[9], (LAYERS, HD), jnp.float32) ** block_scale(splits[9], (LAYERS, HD), ((0, 2),), -0.2, 0.2)), 0.5, 2.0),
        "stale_keys": centred(part_keys[10], (LAYERS, TOKENS, HEADS * HD), 1.0, 6.0, ((0, 2), (2, 8))),
        "stale_values": centred(part_keys[11], (LAYERS, TOKENS, HEADS * HD), 1.0, 6.0, ((0, 2), (2, 8))),
    }


def modulate(hidden, offset, factor):
    values = hidden.astype(jnp.float32)
    center = values - lax.optimization_barrier(jnp.mean(values, axis=-1, keepdims=True))
    spread = lax.optimization_barrier(jnp.mean(center * center, axis=-1, keepdims=True))
    normed = center * lax.rsqrt(spread + 1e-06)
    return (normed * (1.0 + factor) + offset).astype(jnp.bfloat16)

def rms_gain(values, channel_gain):
    scaled = values * lax.rsqrt(lax.optimization_barrier(jnp.mean(values * values, axis=-1, keepdims=True)) + 1e-06)
    return (scaled * channel_gain).astype(jnp.bfloat16)

def attend(queries, key_rows, value_rows):
    head_size = queries.shape[-1]
    scores = jnp.einsum('qhe,khe->hqk', queries.astype(jnp.float32), key_rows.astype(jnp.float32)) / math.sqrt(head_size)
    largest = lax.optimization_barrier(jnp.max(scores, axis=-1, keepdims=True))
    exponent = jnp.exp(scores - largest)
    probs = (exponent / lax.optimization_barrier(jnp.sum(exponent, axis=-1, keepdims=True))).astype(jnp.bfloat16)
    return jnp.einsum('hqk,khe->qhe', probs.astype(jnp.float32), value_rows.astype(jnp.float32)).astype(jnp.bfloat16)

def reference(hidden_in, assign, order, w_qkv, w_out, mod_shift, mod_scale, mod_gate, q_gain, k_gain, stale_keys, stale_values):
    model_width = hidden_in.shape[1]
    head_size = q_gain.shape[1]
    head_count = stale_keys.shape[2] // head_size
    tokens = assign.shape[0]
    patch_count = order.shape[0]
    patch_rows = tokens // patch_count
    owners = assign.reshape(patch_count, patch_rows)
    states = hidden_in[assign].reshape(patch_count, patch_rows, model_width)
    outputs = []
    key_list = []
    value_list = []
    for layer_index in range(stale_keys.shape[0]):
        key_cache = stale_keys[layer_index]
        value_cache = stale_values[layer_index]
        weights = w_qkv[layer_index].reshape(model_width, 3 * head_count * head_size)
        for position in range(patch_count):
            patch_id = order[position]
            current = states[patch_id]
            normed = modulate(current, mod_shift[layer_index], mod_scale[layer_index])
            projected = jnp.dot(normed, weights, preferred_element_type=jnp.float32)
            projected = projected.reshape(patch_rows, 3, head_count, head_size)
            queries = rms_gain(projected[:, 0], q_gain[layer_index])
            fresh_keys = rms_gain(projected[:, 1], k_gain[layer_index])
            fresh_values = projected[:, 2].astype(jnp.bfloat16)
            rows_here = owners[patch_id]
            key_cache = key_cache.at[rows_here].set(fresh_keys.reshape(patch_rows, head_count * head_size))
            value_cache = value_cache.at[rows_here].set(fresh_values.reshape(patch_rows, head_count * head_size))
            attended = attend(queries, key_cache.reshape(tokens, head_count, head_size), value_cache.reshape(tokens, head_count, head_size))
            attended = attended.reshape(patch_rows, head_count * head_size)
            branch = jnp.dot(attended, w_out[layer_index], preferred_element_type=jnp.float32)
            updated = (current.astype(jnp.float32) + mod_gate[layer_index] * branch).astype(jnp.bfloat16)
            states = states.at[patch_id].set(updated)
        outputs.append(states)
        key_list.append(key_cache)
        value_list.append(value_cache)
    return (jnp.stack(outputs), jnp.stack(key_list), jnp.stack(value_list))
```

```python
import math

import jax
import jax.numpy as jnp
from jax import lax
from jax.sharding import PartitionSpec as P


def modulate(hidden, offset, factor):
    values = hidden.astype(jnp.float32)
    center = values - jnp.mean(values, axis=-1, keepdims=True)
    spread = jnp.mean(center * center, axis=-1, keepdims=True)
    normed = center * lax.rsqrt(spread + 1e-06)
    return (normed * (1.0 + factor) + offset).astype(jnp.bfloat16)


def rms_gain(values, channel_gain):
    scaled = values * lax.rsqrt(jnp.mean(values * values, axis=-1, keepdims=True) + 1e-06)
    return (scaled * channel_gain).astype(jnp.bfloat16)


def per_device(
    hidden_in,
    assign,
    order,
    w_qkv,
    w_out,
    mod_shift,
    mod_scale,
    mod_gate,
    q_gain,
    k_gain,
    stale_keys,
    stale_values,
):
    segments = lax.axis_size("segment")
    members = lax.axis_size("ulysses")
    section = lax.axis_index("segment")
    member = lax.axis_index("ulysses")
    width = hidden_in.shape[1]
    head = q_gain.shape[1]
    tokens = assign.shape[0]
    patches = order.shape[0]
    local = tokens // patches // members
    mine = patches * local
    rows = assign.reshape(patches, members, local).transpose(1, 0, 2).reshape(tokens)
    place = jnp.zeros((patches,), jnp.int32).at[order].set(jnp.arange(patches, dtype=jnp.int32))
    turn = jnp.broadcast_to(place[None, :, None], (members, patches, local)).reshape(tokens)
    fresh_seen = turn[None, :] <= turn[:, None]
    weights = w_qkv[0].reshape(width, 3 * head)
    old_keys = stale_keys[0][rows]
    old_values = stale_values[0][rows]

    state = hidden_in[rows]
    own = lax.dynamic_slice_in_dim(state, member * mine, mine)
    result = None
    for step in range(segments):
        normed = modulate(state, mod_shift[0], mod_scale[0])
        projected = jnp.dot(normed, weights, preferred_element_type=jnp.float32)
        queries = rms_gain(projected[:, :head], q_gain[0])
        keys = rms_gain(projected[:, head : 2 * head], k_gain[0])
        values = projected[:, 2 * head :].astype(jnp.bfloat16)
        both = jnp.concatenate([keys, old_keys], axis=0)
        scores = lax.dot_general(
            queries, both, (((1,), (1,)), ((), ())), preferred_element_type=jnp.float32
        )
        scores = jnp.where(fresh_seen, scores[:, :tokens], scores[:, tokens:]) / math.sqrt(head)
        exponent = jnp.exp(scores - jnp.max(scores, axis=-1, keepdims=True))
        probs = (exponent / jnp.sum(exponent, axis=-1, keepdims=True)).astype(jnp.bfloat16)
        none = jnp.zeros_like(probs)
        split = jnp.concatenate(
            [jnp.where(fresh_seen, probs, none), jnp.where(fresh_seen, none, probs)], axis=1
        )
        attended = jnp.dot(
            split, jnp.concatenate([values, old_values], axis=0), preferred_element_type=jnp.float32
        ).astype(jnp.bfloat16)
        share = jnp.dot(attended, w_out[0], preferred_element_type=jnp.float32)
        branch = lax.psum_scatter(
            share.astype(jnp.bfloat16), "ulysses", scatter_dimension=0, tiled=True
        ).astype(jnp.float32)
        updated = (own.astype(jnp.float32) + mod_gate[0] * branch).astype(jnp.bfloat16)
        if result is None:
            result = (updated, keys, values)
        else:
            result = tuple(
                jnp.where(section == step, new, old)
                for new, old in zip((updated, keys, values), result)
            )
        if step + 1 < segments:
            own = lax.ppermute(updated, "segment", [(i, i + 1) for i in range(segments - 1)])
            state = lax.all_gather(own, "ulysses", axis=0, tiled=True)
    updated, keys, values = result
    back = jnp.zeros((tokens,), jnp.int32).at[rows].set(jnp.arange(tokens, dtype=jnp.int32))
    return (updated.reshape(1, patches, local, width), keys[back][None], values[back][None])


def solution(mesh):
    placed = (
        P("rep", None),
        P(),
        P(),
        P("segment", None, None, "ulysses"),
        P("segment", "ulysses", None),
        P("segment", None),
        P("segment", None),
        P("segment", None),
        P("segment", None),
        P("segment", None),
        P("segment", "rep", "ulysses"),
        P("segment", "rep", "ulysses"),
    )
    return jax.shard_map(
        per_device,
        mesh=mesh,
        in_specs=placed,
        out_specs=(
            P("segment", "rep", "ulysses", None),
            P("segment", "rep", "ulysses"),
            P("segment", "rep", "ulysses"),
        ),
        check_vma=False,
    )
```

```python
import functools
import math

import jax
import jax.numpy as jnp
from jax import lax
from jax.experimental import pallas as pl
from jax.experimental.pallas import tpu as pltpu
from jax.sharding import PartitionSpec as P

MESH = pl.DeviceIdType.MESH
CHUNKS = 4


def kernel(
    segments,
    members,
    hidden,
    weights,
    out_rows,
    shift,
    scale,
    gate,
    q_gain,
    k_gain,
    turn_col,
    turn_row,
    rows_col,
    rows_row,
    stale_keys,
    stale_values,
    result,
    new_keys,
    new_values,
    state,
    queries,
    keys,
    values,
    old_keys,
    old_values,
    attended,
    out_cols,
    updated,
    landed,
    load_sem,
    w_send,
    w_recv,
    a_send,
    a_pass,
    a_recv,
    s_send,
    s_pass,
    s_recv,
    o_send,
    o_recv,
):
    fast = 2 if members % 2 == 0 else 1
    slow = members // fast
    section = lax.axis_index("segment")
    me = lax.axis_index("ulysses")
    a, b = me // fast, lax.rem(me, fast)
    tokens, head = stale_keys.shape
    width = members * state.shape[2]
    mine = tokens // members
    chunk = tokens // CHUNKS
    first = section == 0
    last = section == segments - 1

    def remote(src, dst, send, recv, member, where=None):
        return pltpu.make_async_remote_copy(
            src_ref=src,
            dst_ref=dst,
            send_sem=send,
            recv_sem=recv,
            device_id={"segment": section if where is None else where, "ulysses": member},
            device_id_type=MESH,
        )

    def other(step):
        return lax.rem(me + step, members)

    def slow_peer(step):
        return lax.rem(a + step, slow)

    def fast_peer(step):
        return lax.rem(b + step, fast)

    def load():
        return pltpu.make_async_copy(hidden, state, load_sem)

    @pl.when(first)
    def _():
        load().start()

    barrier = pltpu.get_barrier_semaphore()

    def greet(member, where):
        pl.semaphore_signal(
            barrier,
            inc=1,
            device_id={"segment": where, "ulysses": member},
            device_id_type=MESH,
        )

    for step in range(1, members):
        greet(other(step), section)

    @pl.when(jnp.logical_not(last))
    def _():
        for step in range(slow):
            greet(slow_peer(step) * fast + b, section + 1)

    @pl.when(jnp.logical_not(first))
    def _():
        for step in range(slow):
            greet(slow_peer(step) * fast + b, section - 1)

    sides = jnp.where(first, 0, 1) + jnp.where(last, 0, 1)
    pl.semaphore_wait(barrier, members - 1 + slow * sides)

    my_head = pl.ds(pl.multiple_of(me * head, head), head)

    def w_copy(step):
        return remote(
            out_rows.at[other(step)], out_cols.at[my_head], w_send.at[step], w_recv.at[me], other(step)
        )

    def w_arrival(step):
        origin = other(step)
        place = out_cols.at[pl.ds(pl.multiple_of(origin * head, head), head)]
        return remote(place, place, w_send.at[step], w_recv.at[origin], origin)

    for step in range(1, members):
        w_copy(step).start()
    out_cols[my_head, :] = out_rows[me]

    lane = lax.broadcasted_iota(jnp.int32, (tokens, tokens), 1)
    pick = (rows_col[...] == lane).astype(jnp.float32).astype(jnp.bfloat16)
    old_keys[...] = jnp.dot(pick, stale_keys[...], preferred_element_type=jnp.float32).astype(jnp.bfloat16)
    old_values[...] = jnp.dot(pick, stale_values[...], preferred_element_type=jnp.float32).astype(jnp.bfloat16)

    def piece(origin, r):
        return state.at[origin, pl.ds(pl.multiple_of(r * chunk, chunk), chunk)]

    def s_arrival(origin, r):
        place = piece(origin, r)
        return remote(place, place, s_send.at[0, r], s_recv.at[origin, r], other(1))

    def s_forward(origin_slow, step, r):
        origin = origin_slow * fast + b
        place = piece(origin, r)
        return remote(
            place,
            place,
            s_pass.at[origin_slow, step, r],
            s_recv.at[origin, r],
            a * fast + fast_peer(step),
        )

    @pl.when(first)
    def _():
        load().wait()

    def gain(part, factor):
        square = jnp.mean(part * part, axis=-1, keepdims=True)
        return (part * lax.rsqrt(square + 1e-06) * factor).astype(jnp.bfloat16)

    def project(r, carry):
        @pl.when(jnp.logical_not(first))
        def _():
            for step in range(slow):
                origin_slow = slow_peer(step)
                s_arrival(origin_slow * fast + b, r).wait_recv()
                for hop in range(1, fast):
                    s_forward(origin_slow, hop, r).start()
            for hop in range(1, fast):
                for step in range(slow):
                    s_arrival(slow_peer(step) * fast + fast_peer(hop), r).wait_recv()

        rows = pl.ds(pl.multiple_of(r * chunk, chunk), chunk)
        total = jnp.zeros((chunk, 1), jnp.float32)
        for k in range(members):
            total += jnp.sum(state[k, rows].astype(jnp.float32), axis=-1, keepdims=True)
        mean = total / width
        total = jnp.zeros((chunk, 1), jnp.float32)
        for k in range(members):
            center = state[k, rows].astype(jnp.float32) - mean
            total += jnp.sum(center * center, axis=-1, keepdims=True)
        inverse = lax.rsqrt(total / width + 1e-06)
        projected = jnp.zeros((chunk, 3 * head), jnp.float32)
        for k in range(members):
            center = state[k, rows].astype(jnp.float32) - mean
            part = (center * inverse * (1.0 + scale[k]) + shift[k]).astype(jnp.bfloat16)
            projected += jnp.dot(part, weights[k], preferred_element_type=jnp.float32)
        queries[rows, :] = gain(projected[:, :head], q_gain[...])
        keys[rows, :] = gain(projected[:, head : 2 * head], k_gain[...])
        values[rows, :] = projected[:, 2 * head :].astype(jnp.bfloat16)
        return carry

    lax.fori_loop(0, CHUNKS, project, 0)

    def attend(r, carry):
        rows = pl.ds(pl.multiple_of(r * chunk, chunk), chunk)
        seen = turn_row[...] <= turn_col[rows, :]
        across = (((1,), (1,)), ((), ()))
        asked = queries[rows, :]
        scores = jnp.where(
            seen,
            lax.dot_general(asked, keys[...], across, preferred_element_type=jnp.float32),
            lax.dot_general(asked, old_keys[...], across, preferred_element_type=jnp.float32),
        ) / math.sqrt(head)
        exponent = jnp.exp(scores - jnp.max(scores, axis=-1, keepdims=True))
        probs = exponent / jnp.sum(exponent, axis=-1, keepdims=True)
        fresh = jnp.where(seen, probs, 0.0).astype(jnp.bfloat16)
        stale = jnp.where(seen, 0.0, probs).astype(jnp.bfloat16)
        attended[rows, my_head] = (
            jnp.dot(fresh, values[...], preferred_element_type=jnp.float32)
            + jnp.dot(stale, old_values[...], preferred_element_type=jnp.float32)
        ).astype(jnp.bfloat16)
        return carry

    lax.fori_loop(0, CHUNKS, attend, 0)

    def heads(origin):
        return attended.at[:, pl.ds(pl.multiple_of(origin * head, head), head)]

    def a_copy(step):
        place = heads(me)
        return remote(place, place, a_send.at[step], a_recv.at[me], slow_peer(step) * fast + b)

    def a_forward(origin_slow, step):
        origin = origin_slow * fast + b
        place = heads(origin)
        return remote(
            place, place, a_pass.at[origin_slow, step], a_recv.at[origin], a * fast + fast_peer(step)
        )

    def a_arrival(origin):
        place = heads(origin)
        return remote(place, place, a_send.at[0], a_recv.at[origin], other(1))

    for step in range(1, slow):
        a_copy(step).start()
    for hop in range(1, fast):
        a_forward(a, hop).start()

    row = lax.broadcasted_iota(jnp.int32, (tokens, tokens), 0)
    put = (rows_row[...] == row).astype(jnp.float32).astype(jnp.bfloat16)
    new_keys[...] = jnp.dot(put, keys[...], preferred_element_type=jnp.float32).astype(jnp.bfloat16)
    new_values[...] = jnp.dot(put, values[...], preferred_element_type=jnp.float32).astype(jnp.bfloat16)

    for step in range(1, slow):
        origin_slow = slow_peer(step)
        a_arrival(origin_slow * fast + b).wait_recv()
        for hop in range(1, fast):
            a_forward(origin_slow, hop).start()
    for step in range(1, members):
        w_arrival(step).wait_recv()
    for hop in range(1, fast):
        for step in range(slow):
            a_arrival(slow_peer(step) * fast + fast_peer(hop)).wait_recv()

    def s_copy(step, r):
        rows = pl.ds(pl.multiple_of(r * chunk, chunk), chunk)
        return remote(
            updated.at[rows],
            piece(me, r),
            s_send.at[step, r],
            s_recv.at[me, r],
            slow_peer(step) * fast + b,
            section + 1,
        )

    def finish(r, carry):
        rows = pl.ds(pl.multiple_of(r * chunk, chunk), chunk)
        branch = jnp.dot(attended[rows, :], out_cols[...], preferred_element_type=jnp.float32)
        updated[rows, :] = (state[me, rows].astype(jnp.float32) + gate[me] * branch).astype(jnp.bfloat16)

        @pl.when(jnp.logical_not(last))
        def _():
            for step in range(slow):
                s_copy(step, r).start()

        return carry

    lax.fori_loop(0, CHUNKS, finish, 0)

    def o_copy(step):
        target = other(step)
        return remote(
            updated.at[pl.ds(pl.multiple_of(target * mine, mine), mine)],
            landed.at[me],
            o_send.at[step],
            o_recv.at[me],
            target,
        )

    def o_arrival(step):
        origin = other(step)
        return remote(landed.at[origin], landed.at[origin], o_send.at[step], o_recv.at[origin], origin)

    for step in range(1, members):
        o_copy(step).start()
    landed[me] = updated[pl.ds(pl.multiple_of(me * mine, mine), mine), :]

    for step in range(1, members):
        w_copy(step).wait_send()
    for step in range(1, slow):
        a_copy(step).wait_send()
    for hop in range(1, fast):
        for step in range(slow):
            a_forward(slow_peer(step), hop).wait_send()

    def drain(r, carry):
        @pl.when(jnp.logical_not(last))
        def _():
            for step in range(slow):
                s_copy(step, r).wait_send()

        @pl.when(jnp.logical_not(first))
        def _():
            for step in range(slow):
                for hop in range(1, fast):
                    s_forward(slow_peer(step), hop, r).wait_send()

        return carry

    lax.fori_loop(0, CHUNKS, drain, 0)
    for step in range(1, members):
        o_arrival(step).wait_recv()
    for step in range(1, members):
        o_copy(step).wait_send()
    result[...] = landed[...]


def per_device(
    hidden_in,
    assign,
    order,
    w_qkv,
    w_out,
    mod_shift,
    mod_scale,
    mod_gate,
    q_gain,
    k_gain,
    stale_keys,
    stale_values,
):
    segments = lax.axis_size("segment")
    members = lax.axis_size("ulysses")
    width = hidden_in.shape[1]
    head = q_gain.shape[1]
    tokens = assign.shape[0]
    patches = order.shape[0]
    local = tokens // patches // members
    mine = patches * local
    part = width // members
    fast = 2 if members % 2 == 0 else 1
    slow = members // fast
    rows = assign.reshape(patches, members, local).transpose(1, 0, 2).reshape(tokens)
    place = jnp.sum(
        jnp.where(
            order[None, :] == jnp.arange(patches, dtype=jnp.int32)[:, None],
            jnp.arange(patches, dtype=jnp.int32)[None, :],
            0,
        ),
        axis=1,
    )
    turn = jnp.broadcast_to(place[None, :, None], (members, patches, local)).reshape(tokens)
    hidden = hidden_in[rows].reshape(tokens, members, part).transpose(1, 0, 2)
    weights = w_qkv[0].reshape(members, part, 3 * head)
    out_rows = w_out[0].reshape(head, members, part).transpose(1, 0, 2)
    bf16 = jnp.bfloat16
    inside = pl.BlockSpec(memory_space=pltpu.VMEM)
    dma = pltpu.SemaphoreType.DMA
    result, new_keys, new_values = pl.pallas_call(
        functools.partial(kernel, segments, members),
        out_shape=(
            jax.ShapeDtypeStruct((members, mine, part), bf16),
            jax.ShapeDtypeStruct((tokens, head), bf16),
            jax.ShapeDtypeStruct((tokens, head), bf16),
        ),
        in_specs=[pl.BlockSpec(memory_space=pl.ANY)] + [inside] * 13,
        out_specs=(inside, inside, inside),
        scratch_shapes=[
            pltpu.VMEM((members, tokens, part), bf16),
            pltpu.VMEM((tokens, head), bf16),
            pltpu.VMEM((tokens, head), bf16),
            pltpu.VMEM((tokens, head), bf16),
            pltpu.VMEM((tokens, head), bf16),
            pltpu.VMEM((tokens, head), bf16),
            pltpu.VMEM((tokens, members * head), bf16),
            pltpu.VMEM((members * head, part), bf16),
            pltpu.VMEM((tokens, part), bf16),
            pltpu.VMEM((members, mine, part), bf16),
            dma(()),
            dma((members,)),
            dma((members,)),
            dma((slow,)),
            dma((slow, fast)),
            dma((members,)),
            dma((slow, CHUNKS)),
            dma((slow, fast, CHUNKS)),
            dma((members, CHUNKS)),
            dma((members,)),
            dma((members,)),
        ],
        compiler_params=pltpu.CompilerParams(
            collective_id=0, has_side_effects=True, vmem_limit_bytes=40 * 2**20
        ),
        cost_estimate=pl.CostEstimate(
            flops=2 * tokens * width * 4 * head, bytes_accessed=10**7, transcendentals=tokens * tokens
        ),
    )(
        hidden,
        weights,
        out_rows,
        mod_shift.reshape(members, 1, part),
        mod_scale.reshape(members, 1, part),
        mod_gate.reshape(members, 1, part),
        q_gain,
        k_gain,
        turn[:, None],
        turn[None, :],
        rows[:, None],
        rows[None, :],
        stale_keys[0],
        stale_values[0],
    )
    block_out = result.transpose(1, 0, 2).reshape(1, patches, local, width)
    return (block_out, new_keys[None], new_values[None])


def solution(mesh):
    placed = (
        P("rep", None),
        P(),
        P(),
        P("segment", None, None, "ulysses"),
        P("segment", "ulysses", None),
        P("segment", None),
        P("segment", None),
        P("segment", None),
        P("segment", None),
        P("segment", None),
        P("segment", "rep", "ulysses"),
        P("segment", "rep", "ulysses"),
    )
    return jax.shard_map(
        per_device,
        mesh=mesh,
        in_specs=placed,
        out_specs=(
            P("segment", "rep", "ulysses", None),
            P("segment", "rep", "ulysses"),
            P("segment", "rep", "ulysses"),
        ),
        check_vma=False,
    )
```

```python
import functools
import math

import jax
import jax.numpy as jnp
from jax import lax
from jax.experimental import pallas as pl
from jax.experimental.pallas import tpu as pltpu
from jax.sharding import PartitionSpec as P

MESH = pl.DeviceIdType.MESH
CHUNKS = 4


def kernel(
    segments,
    members,
    patches,
    order,
    weights,
    hidden,
    out_rows,
    shift_in,
    scale_in,
    gate_in,
    q_gain_in,
    k_gain_in,
    assign_in,
    stale_keys_in,
    stale_values_in,
    result,
    new_keys,
    new_values,
    raw,
    state,
    pick,
    queries,
    keys,
    values,
    stale_keys,
    stale_values,
    old_keys,
    old_values,
    shift,
    scale,
    gate,
    q_gain,
    k_gain,
    assign,
    attended,
    out_cols,
    updated,
    landed,
    load_sem,
    raw_sem,
    w_send,
    w_recv,
    w_pass,
    w_twin,
    a_send,
    a_pass,
    a_recv,
    s_send,
    s_pass,
    s_recv,
    o_send,
    o_recv,
):
    fast = 2 if members % 2 == 0 else 1
    slow = members // fast
    section = lax.axis_index("segment")
    me = lax.axis_index("ulysses")
    core = lax.axis_index("rep")
    a, b = me // fast, lax.rem(me, fast)
    tokens, head = stale_keys.shape
    part = state.shape[2]
    width = members * part
    half = head // 2
    aligned = part % 128 == 0
    mine = tokens // members
    chunk = tokens // CHUNKS
    first = section == 0
    last = section == segments - 1

    def columns(ref, index):
        if not aligned:
            return ref.at[index]
        return ref.at[:, pl.ds(pl.multiple_of(index * part, 128), part)]

    def remote(src, dst, send, recv, member, where=None):
        return pltpu.make_async_remote_copy(
            src_ref=src,
            dst_ref=dst,
            send_sem=send,
            recv_sem=recv,
            device_id={"segment": section if where is None else where, "ulysses": member},
            device_id_type=MESH,
        )

    def other(step):
        return lax.rem(me + step, members)

    def slow_peer(step):
        return lax.rem(a + step, slow)

    def fast_peer(step):
        return lax.rem(b + step, fast)

    my_head = pl.ds(pl.multiple_of(me * head, head), head)
    loads = [
        pltpu.make_async_copy(src, dst, load_sem.at[i])
        for i, (src, dst) in enumerate(
            (
                (assign_in, assign),
                (stale_keys_in, stale_keys),
                (stale_values_in, stale_values),
                (shift_in, shift),
                (scale_in, scale),
                (q_gain_in, q_gain),
                (k_gain_in, k_gain),
                (gate_in, gate),
                (columns(out_rows, me), out_cols.at[my_head]),
            )
        )
    ]

    def load_raw(k):
        return pltpu.make_async_copy(columns(hidden, k), raw.at[k], raw_sem.at[k])

    for copy in loads:
        copy.start()

    @pl.when(first)
    def _():
        for k in range(members):
            load_raw(k).start()

    barrier = pltpu.get_barrier_semaphore()

    def greet(member, where):
        pl.semaphore_signal(
            barrier,
            inc=1,
            device_id={"segment": where, "ulysses": member},
            device_id_type=MESH,
        )

    for step in range(1, members):
        greet(other(step), section)

    @pl.when(jnp.logical_not(last))
    def _():
        for step in range(slow):
            greet(slow_peer(step) * fast + b, section + 1)

    @pl.when(jnp.logical_not(first))
    def _():
        for step in range(slow):
            greet(slow_peer(step) * fast + b, section - 1)

    pl.semaphore_signal(
        barrier, inc=1, device_id={"rep": 1 - core}, device_id_type=MESH
    )
    sides = jnp.where(first, 0, 1) + jnp.where(last, 0, 1)
    pl.semaphore_wait(barrier, members + slow * sides)

    def w_place(origin, which):
        return out_cols.at[pl.ds(pl.multiple_of(origin * head + which * half, half), half)]

    def w_copy(step):
        target = other(step)
        rows = pl.ds(pl.multiple_of(core * half, half), half)
        if aligned:
            piece = out_rows.at[rows, pl.ds(pl.multiple_of(target * part, 128), part)]
        else:
            piece = out_rows.at[target, rows]
        return remote(piece, w_place(me, core), w_send.at[step], w_recv.at[me], target)

    def w_arrival(step):
        origin = other(step)
        place = w_place(origin, core)
        return remote(place, place, w_send.at[step], w_recv.at[origin], origin)

    def twin_copy(step, which):
        origin = other(step)
        place = w_place(origin, which)
        return pltpu.make_async_remote_copy(
            src_ref=place,
            dst_ref=place,
            send_sem=w_pass.at[step],
            recv_sem=w_twin.at[origin],
            device_id={"rep": 1 - core},
            device_id_type=MESH,
        )

    for step in range(1, members):
        w_copy(step).start()

    mine_rows = tokens // members
    local = mine_rows // patches

    def turns(index):
        patch = lax.rem(index // local, patches)
        total = jnp.zeros_like(index)
        for i in range(patches):
            total += jnp.where(patch == order[i], i, 0)
        return total

    lane = lax.broadcasted_iota(jnp.int32, (tokens, tokens), 1)
    row = lax.broadcasted_iota(jnp.int32, (tokens, 1), 0)
    source = lax.rem(row // local, patches) * (tokens // patches) + row // mine_rows * local + lax.rem(row, local)
    for copy in loads[:1]:
        copy.wait()
    chosen = jnp.sum(jnp.where(lane == source, assign[...].astype(jnp.float32), 0.0), axis=1, keepdims=True)
    pick[...] = (lane.astype(jnp.float32) == chosen).astype(jnp.float32).astype(jnp.bfloat16)
    for copy in loads[1:]:
        copy.wait()

    def exact(mask, data):
        return jnp.dot(mask, data, preferred_element_type=jnp.float32).astype(jnp.bfloat16)

    old_keys[...] = exact(pick[...], stale_keys[...])
    old_values[...] = exact(pick[...], stale_values[...])

    def piece(origin, r):
        return state.at[origin, pl.ds(pl.multiple_of(r * chunk, chunk), chunk)]

    def s_arrival(origin, r):
        place = piece(origin, r)
        return remote(place, place, s_send.at[0, r], s_recv.at[origin, r], other(1))

    def s_forward(origin_slow, step, r):
        origin = origin_slow * fast + b
        place = piece(origin, r)
        return remote(
            place,
            place,
            s_pass.at[origin_slow, step, r],
            s_recv.at[origin, r],
            a * fast + fast_peer(step),
        )

    @pl.when(first)
    def _():
        for k in range(members):
            load_raw(k).wait()

    def gain(data, factor):
        square = jnp.mean(data * data, axis=-1, keepdims=True)
        return (data * lax.rsqrt(square + 1e-06) * factor).astype(jnp.bfloat16)

    def vector(ref, k):
        return ref[:, k * part : (k + 1) * part] if aligned else ref[k]

    def project(r, carry):
        @pl.when(jnp.logical_not(first))
        def _():
            for step in range(slow):
                origin_slow = slow_peer(step)
                s_arrival(origin_slow * fast + b, r).wait_recv()
                for hop in range(1, fast):
                    s_forward(origin_slow, hop, r).start()
            for hop in range(1, fast):
                for step in range(slow):
                    s_arrival(slow_peer(step) * fast + fast_peer(hop), r).wait_recv()

        rows = pl.ds(pl.multiple_of(r * chunk, chunk), chunk)

        @pl.when(first)
        def _():
            for k in range(members):
                state[k, rows] = exact(pick[rows, :], raw[k])

        total = jnp.zeros((chunk, 1), jnp.float32)
        for k in range(members):
            total += jnp.sum(state[k, rows].astype(jnp.float32), axis=-1, keepdims=True)
        mean = total / width
        total = jnp.zeros((chunk, 1), jnp.float32)
        for k in range(members):
            center = state[k, rows].astype(jnp.float32) - mean
            total += jnp.sum(center * center, axis=-1, keepdims=True)
        inverse = lax.rsqrt(total / width + 1e-06)
        projected = jnp.zeros((chunk, 3 * head), jnp.float32)
        for k in range(members):
            center = state[k, rows].astype(jnp.float32) - mean
            normed = (center * inverse * (1.0 + vector(scale, k)) + vector(shift, k)).astype(jnp.bfloat16)
            projected += jnp.dot(
                normed, weights[k * part : (k + 1) * part, :], preferred_element_type=jnp.float32
            )
        queries[rows, :] = gain(projected[:, :head], q_gain[...])
        keys[rows, :] = gain(projected[:, head : 2 * head], k_gain[...])
        values[rows, :] = projected[:, 2 * head :].astype(jnp.bfloat16)
        return carry

    lax.fori_loop(0, CHUNKS, project, 0)

    def attend(r, carry):
        rows = pl.ds(pl.multiple_of(r * chunk, chunk), chunk)
        asking = lax.broadcasted_iota(jnp.int32, (chunk, tokens), 0) + r * chunk
        asked_of = lax.broadcasted_iota(jnp.int32, (chunk, tokens), 1)
        seen = turns(asked_of) <= turns(asking)
        across = (((1,), (1,)), ((), ()))
        asked = queries[rows, :]
        scores = jnp.where(
            seen,
            lax.dot_general(asked, keys[...], across, preferred_element_type=jnp.float32),
            lax.dot_general(asked, old_keys[...], across, preferred_element_type=jnp.float32),
        ) / math.sqrt(head)
        exponent = jnp.exp(scores - jnp.max(scores, axis=-1, keepdims=True))
        probs = exponent / jnp.sum(exponent, axis=-1, keepdims=True)
        fresh = jnp.where(seen, probs, 0.0).astype(jnp.bfloat16)
        stale = jnp.where(seen, 0.0, probs).astype(jnp.bfloat16)
        attended[rows, my_head] = (
            jnp.dot(fresh, values[...], preferred_element_type=jnp.float32)
            + jnp.dot(stale, old_values[...], preferred_element_type=jnp.float32)
        ).astype(jnp.bfloat16)
        return carry

    lax.fori_loop(0, CHUNKS, attend, 0)

    def heads(origin):
        return attended.at[:, pl.ds(pl.multiple_of(origin * head, head), head)]

    def a_copy(step):
        place = heads(me)
        return remote(place, place, a_send.at[step], a_recv.at[me], slow_peer(step) * fast + b)

    def a_forward(origin_slow, step):
        origin = origin_slow * fast + b
        place = heads(origin)
        return remote(
            place, place, a_pass.at[origin_slow, step], a_recv.at[origin], a * fast + fast_peer(step)
        )

    def a_arrival(origin):
        place = heads(origin)
        return remote(place, place, a_send.at[0], a_recv.at[origin], other(1))

    for step in range(1, slow):
        a_copy(step).start()
    for hop in range(1, fast):
        a_forward(a, hop).start()

    back = (((0,), (0,)), ((), ()))
    new_keys[...] = lax.dot_general(
        pick[...], keys[...], back, preferred_element_type=jnp.float32
    ).astype(jnp.bfloat16)
    new_values[...] = lax.dot_general(
        pick[...], values[...], back, preferred_element_type=jnp.float32
    ).astype(jnp.bfloat16)

    for step in range(1, slow):
        origin_slow = slow_peer(step)
        a_arrival(origin_slow * fast + b).wait_recv()
        for hop in range(1, fast):
            a_forward(origin_slow, hop).start()
    for step in range(1, members):
        w_arrival(step).wait_recv()
        twin_copy(step, core).start()
    for hop in range(1, fast):
        for step in range(slow):
            a_arrival(slow_peer(step) * fast + fast_peer(hop)).wait_recv()
    for step in range(1, members):
        twin_copy(step, 1 - core).wait_recv()
    my_gate = gate[:, pl.ds(pl.multiple_of(me * part, 128), part)] if aligned else gate[me]

    def s_copy(step, r):
        rows = pl.ds(pl.multiple_of(r * chunk, chunk), chunk)
        return remote(
            updated.at[rows],
            piece(me, r),
            s_send.at[step, r],
            s_recv.at[me, r],
            slow_peer(step) * fast + b,
            section + 1,
        )

    def finish(r, carry):
        rows = pl.ds(pl.multiple_of(r * chunk, chunk), chunk)
        branch = jnp.dot(attended[rows, :], out_cols[...], preferred_element_type=jnp.float32)
        updated[rows, :] = (state[me, rows].astype(jnp.float32) + my_gate * branch).astype(jnp.bfloat16)

        @pl.when(jnp.logical_not(last))
        def _():
            for step in range(slow):
                s_copy(step, r).start()

        return carry

    lax.fori_loop(0, CHUNKS, finish, 0)

    def o_copy(step):
        target = other(step)
        return remote(
            updated.at[pl.ds(pl.multiple_of(target * mine, mine), mine)],
            landed.at[me],
            o_send.at[step],
            o_recv.at[me],
            target,
        )

    def o_arrival(step):
        origin = other(step)
        return remote(landed.at[origin], landed.at[origin], o_send.at[step], o_recv.at[origin], origin)

    for step in range(1, members):
        o_copy(step).start()
    landed[me] = updated[pl.ds(pl.multiple_of(me * mine, mine), mine), :]

    for step in range(1, members):
        w_copy(step).wait_send()
        twin_copy(step, core).wait_send()
    for step in range(1, slow):
        a_copy(step).wait_send()
    for hop in range(1, fast):
        for step in range(slow):
            a_forward(slow_peer(step), hop).wait_send()

    def drain(r, carry):
        @pl.when(jnp.logical_not(last))
        def _():
            for step in range(slow):
                s_copy(step, r).wait_send()

        @pl.when(jnp.logical_not(first))
        def _():
            for step in range(slow):
                for hop in range(1, fast):
                    s_forward(slow_peer(step), hop, r).wait_send()

        return carry

    lax.fori_loop(0, CHUNKS, drain, 0)
    for step in range(1, members):
        o_arrival(step).wait_recv()
    for step in range(1, members):
        o_copy(step).wait_send()
    if aligned:
        for k in range(members):
            result[:, k * part : (k + 1) * part] = landed[k]
    else:
        result[...] = landed[...]


def per_device(
    hidden_in,
    assign,
    order,
    w_qkv,
    w_out,
    mod_shift,
    mod_scale,
    mod_gate,
    q_gain,
    k_gain,
    stale_keys,
    stale_values,
):
    segments = lax.axis_size("segment")
    members = lax.axis_size("ulysses")
    width = hidden_in.shape[1]
    head = q_gain.shape[1]
    tokens = assign.shape[0]
    patches = order.shape[0]
    local = tokens // patches // members
    mine = patches * local
    part = width // members
    fast = 2 if members % 2 == 0 else 1
    slow = members // fast
    aligned = part % 128 == 0

    def blocks(array):
        if aligned:
            return array
        return array.reshape(array.shape[0], members, part).transpose(1, 0, 2)

    vectors = (1, width) if aligned else (members, 1, part)
    shaped = (mine, width) if aligned else (members, mine, part)
    bf16 = jnp.bfloat16
    inside = pl.BlockSpec(memory_space=pltpu.VMEM)
    dma = pltpu.SemaphoreType.DMA
    result, new_keys, new_values = pl.pallas_call(
        functools.partial(kernel, segments, members, patches),
        out_shape=(
            jax.ShapeDtypeStruct(shaped, bf16),
            jax.ShapeDtypeStruct((tokens, head), bf16),
            jax.ShapeDtypeStruct((tokens, head), bf16),
        ),
        in_specs=[pl.BlockSpec(memory_space=pltpu.SMEM), inside] + [pl.BlockSpec(memory_space=pl.ANY)] * 10,
        out_specs=(inside, inside, inside),
        scratch_shapes=[
            pltpu.VMEM((members, tokens, part), bf16),
            pltpu.VMEM((members, tokens, part), bf16),
            pltpu.VMEM((tokens, tokens), bf16),
        ]
        + [pltpu.VMEM((tokens, head), bf16)] * 7
        + [pltpu.VMEM(vectors, jnp.float32)] * 3
        + [pltpu.VMEM((1, head), jnp.float32)] * 2
        + [
            pltpu.VMEM((1, tokens), jnp.int32),
            pltpu.VMEM((tokens, members * head), bf16),
            pltpu.VMEM((members * head, part), bf16),
            pltpu.VMEM((tokens, part), bf16),
            pltpu.VMEM((members, mine, part), bf16),
            dma((9,)),
            dma((members,)),
            dma((members,)),
            dma((members,)),
            dma((members,)),
            dma((members,)),
            dma((slow,)),
            dma((slow, fast)),
            dma((members,)),
            dma((slow, CHUNKS)),
            dma((slow, fast, CHUNKS)),
            dma((members, CHUNKS)),
            dma((members,)),
            dma((members,)),
        ],
        compiler_params=pltpu.CompilerParams(
            collective_id=0, has_side_effects=True, vmem_limit_bytes=40 * 2**20
        ),
        cost_estimate=pl.CostEstimate(
            flops=2 * tokens * width * 4 * head, bytes_accessed=10**7, transcendentals=tokens * tokens
        ),
    )(
        order,
        w_qkv[0].reshape(width, 3 * head),
        blocks(hidden_in),
        blocks(w_out[0]),
        blocks(mod_shift),
        blocks(mod_scale),
        blocks(mod_gate),
        q_gain,
        k_gain,
        assign[None, :],
        stale_keys[0],
        stale_values[0],
    )
    if not aligned:
        result = result.transpose(1, 0, 2)
    block_out = result.reshape(1, patches, local, width)
    return (block_out, new_keys[None], new_values[None])


def solution(mesh):
    placed = (
        P("rep", None),
        P(),
        P(),
        P("segment", None, None, "ulysses"),
        P("segment", "ulysses", None),
        P("segment", None),
        P("segment", None),
        P("segment", None),
        P("segment", None),
        P("segment", None),
        P("segment", "rep", "ulysses"),
        P("segment", "rep", "ulysses"),
    )
    return jax.shard_map(
        per_device,
        mesh=mesh,
        in_specs=placed,
        out_specs=(
            P("segment", "rep", "ulysses", None),
            P("segment", "rep", "ulysses"),
            P("segment", "rep", "ulysses"),
        ),
        check_vma=False,
    )
```

```python
import functools
import math

import jax
import jax.numpy as jnp
from jax import lax
from jax.experimental import pallas as pl
from jax.experimental.pallas import tpu as pltpu
from jax.sharding import PartitionSpec as P

MESH = pl.DeviceIdType.MESH
CHUNKS = 4


def kernel(
    segments,
    members,
    patches,
    order,
    weights_in,
    hidden,
    out_rows,
    shift_in,
    scale_in,
    gate_in,
    q_gain_in,
    k_gain_in,
    assign_in,
    stale_keys_in,
    stale_values_in,
    result,
    new_keys,
    new_values,
    weights,
    raw,
    state,
    pick,
    queries,
    keys,
    values,
    stale_keys,
    stale_values,
    old_keys,
    old_values,
    shift,
    scale,
    gate,
    q_gain,
    k_gain,
    assign,
    attended,
    out_cols,
    updated,
    landed,
    load_sem,
    wide_sem,
    raw_sem,
    w_send,
    w_recv,
    w_pass,
    w_twin,
    a_send,
    a_pass,
    a_recv,
    s_send,
    s_pass,
    s_recv,
    o_send,
    o_recv,
):
    fast = 2 if members % 2 == 0 else 1
    slow = members // fast
    section = lax.axis_index("segment")
    me = lax.axis_index("ulysses")
    core = lax.axis_index("rep")
    a, b = me // fast, lax.rem(me, fast)
    tokens, head = stale_keys.shape
    part = state.shape[2]
    width = members * part
    half = head // 2
    aligned = part % 128 == 0
    mine = tokens // members
    chunk = tokens // CHUNKS
    first = section == 0
    last = section == segments - 1

    def columns(ref, index):
        if not aligned:
            return ref.at[index]
        return ref.at[:, pl.ds(pl.multiple_of(index * part, 128), part)]

    def remote(src, dst, send, recv, member, where=None):
        return pltpu.make_async_remote_copy(
            src_ref=src,
            dst_ref=dst,
            send_sem=send,
            recv_sem=recv,
            device_id={"segment": section if where is None else where, "ulysses": member},
            device_id_type=MESH,
        )

    def other(step):
        return lax.rem(me + step, members)

    def slow_peer(step):
        return lax.rem(a + step, slow)

    def fast_peer(step):
        return lax.rem(b + step, fast)

    my_head = pl.ds(pl.multiple_of(me * head, head), head)
    loads = [
        pltpu.make_async_copy(src, dst, load_sem.at[i])
        for i, (src, dst) in enumerate(
            (
                (assign_in, assign),
                (stale_keys_in, stale_keys),
                (stale_values_in, stale_values),
                (shift_in, shift),
                (scale_in, scale),
                (q_gain_in, q_gain),
                (k_gain_in, k_gain),
                (gate_in, gate),
                (columns(out_rows, me), out_cols.at[my_head]),
            )
        )
    ]

    wide_loads = [
        pltpu.make_async_copy(
            weights_in.at[j], weights.at[:, pl.ds(j * head, head)], wide_sem.at[j]
        )
        for j in range(3)
    ]

    def load_raw(k):
        return pltpu.make_async_copy(columns(hidden, k), raw.at[k], raw_sem.at[k])

    for copy in loads:
        copy.start()

    @pl.when(first)
    def _():
        for k in range(members):
            load_raw(k).start()

    for copy in wide_loads:
        copy.start()

    barrier = pltpu.get_barrier_semaphore()

    def greet(member, where):
        pl.semaphore_signal(
            barrier,
            inc=1,
            device_id={"segment": where, "ulysses": member},
            device_id_type=MESH,
        )

    for step in range(1, members):
        greet(other(step), section)

    @pl.when(jnp.logical_not(last))
    def _():
        for step in range(slow):
            greet(slow_peer(step) * fast + b, section + 1)

    @pl.when(jnp.logical_not(first))
    def _():
        for step in range(slow):
            greet(slow_peer(step) * fast + b, section - 1)

    pl.semaphore_signal(
        barrier, inc=1, device_id={"rep": 1 - core}, device_id_type=MESH
    )
    sides = jnp.where(first, 0, 1) + jnp.where(last, 0, 1)
    pl.semaphore_wait(barrier, members + slow * sides)

    def w_place(origin, which):
        return out_cols.at[pl.ds(pl.multiple_of(origin * head + which * half, half), half)]

    def w_copy(step):
        target = other(step)
        rows = pl.ds(pl.multiple_of(core * half, half), half)
        if aligned:
            piece = out_rows.at[rows, pl.ds(pl.multiple_of(target * part, 128), part)]
        else:
            piece = out_rows.at[target, rows]
        return remote(piece, w_place(me, core), w_send.at[step], w_recv.at[me], target)

    def w_arrival(step):
        origin = other(step)
        place = w_place(origin, core)
        return remote(place, place, w_send.at[step], w_recv.at[origin], origin)

    def twin_copy(step, which):
        origin = other(step)
        place = w_place(origin, which)
        return pltpu.make_async_remote_copy(
            src_ref=place,
            dst_ref=place,
            send_sem=w_pass.at[step],
            recv_sem=w_twin.at[origin],
            device_id={"rep": 1 - core},
            device_id_type=MESH,
        )

    for step in range(1, members):
        w_copy(step).start()

    mine_rows = tokens // members
    local = mine_rows // patches

    def turns(index):
        patch = lax.rem(index // local, patches)
        total = jnp.zeros_like(index)
        for i in range(patches):
            total += jnp.where(patch == order[i], i, 0)
        return total

    lane = lax.broadcasted_iota(jnp.int32, (tokens, tokens), 1)
    row = lax.broadcasted_iota(jnp.int32, (tokens, 1), 0)
    source = lax.rem(row // local, patches) * (tokens // patches) + row // mine_rows * local + lax.rem(row, local)
    for copy in loads[:1]:
        copy.wait()
    chosen = jnp.sum(jnp.where(lane == source, assign[...].astype(jnp.float32), 0.0), axis=1, keepdims=True)
    pick[...] = (lane.astype(jnp.float32) == chosen).astype(jnp.float32).astype(jnp.bfloat16)
    for copy in loads[1:]:
        copy.wait()

    def exact(mask, data):
        return jnp.dot(mask, data, preferred_element_type=jnp.float32).astype(jnp.bfloat16)

    old_keys[...] = exact(pick[...], stale_keys[...])
    old_values[...] = exact(pick[...], stale_values[...])

    def piece(origin, r):
        return state.at[origin, pl.ds(pl.multiple_of(r * chunk, chunk), chunk)]

    def s_arrival(origin, r):
        place = piece(origin, r)
        return remote(place, place, s_send.at[0, r], s_recv.at[origin, r], other(1))

    def s_forward(origin_slow, step, r):
        origin = origin_slow * fast + b
        place = piece(origin, r)
        return remote(
            place,
            place,
            s_pass.at[origin_slow, step, r],
            s_recv.at[origin, r],
            a * fast + fast_peer(step),
        )

    @pl.when(first)
    def _():
        for k in range(members):
            load_raw(k).wait()

    for copy in wide_loads:
        copy.wait()

    def gain(data, factor):
        square = jnp.mean(data * data, axis=-1, keepdims=True)
        return (data * lax.rsqrt(square + 1e-06) * factor).astype(jnp.bfloat16)

    def vector(ref, k):
        return ref[:, k * part : (k + 1) * part] if aligned else ref[k]

    def project(r, carry):
        @pl.when(jnp.logical_not(first))
        def _():
            for step in range(slow):
                origin_slow = slow_peer(step)
                s_arrival(origin_slow * fast + b, r).wait_recv()
                for hop in range(1, fast):
                    s_forward(origin_slow, hop, r).start()
            for hop in range(1, fast):
                for step in range(slow):
                    s_arrival(slow_peer(step) * fast + fast_peer(hop), r).wait_recv()

        rows = pl.ds(pl.multiple_of(r * chunk, chunk), chunk)

        @pl.when(first)
        def _():
            for k in range(members):
                state[k, rows] = exact(pick[rows, :], raw[k])

        total = jnp.zeros((chunk, 1), jnp.float32)
        for k in range(members):
            total += jnp.sum(state[k, rows].astype(jnp.float32), axis=-1, keepdims=True)
        mean = total / width
        total = jnp.zeros((chunk, 1), jnp.float32)
        for k in range(members):
            center = state[k, rows].astype(jnp.float32) - mean
            total += jnp.sum(center * center, axis=-1, keepdims=True)
        inverse = lax.rsqrt(total / width + 1e-06)
        projected = jnp.zeros((chunk, 3 * head), jnp.float32)
        for k in range(members):
            center = state[k, rows].astype(jnp.float32) - mean
            normed = (center * inverse * (1.0 + vector(scale, k)) + vector(shift, k)).astype(jnp.bfloat16)
            projected += jnp.dot(
                normed, weights[k * part : (k + 1) * part, :], preferred_element_type=jnp.float32
            )
        queries[rows, :] = gain(projected[:, :head], q_gain[...])
        keys[rows, :] = gain(projected[:, head : 2 * head], k_gain[...])
        values[rows, :] = projected[:, 2 * head :].astype(jnp.bfloat16)
        return carry

    lax.fori_loop(0, CHUNKS, project, 0)

    def attend(r, carry):
        rows = pl.ds(pl.multiple_of(r * chunk, chunk), chunk)
        asking = lax.broadcasted_iota(jnp.int32, (chunk, tokens), 0) + r * chunk
        asked_of = lax.broadcasted_iota(jnp.int32, (chunk, tokens), 1)
        seen = turns(asked_of) <= turns(asking)
        across = (((1,), (1,)), ((), ()))
        asked = queries[rows, :]
        scores = jnp.where(
            seen,
            lax.dot_general(asked, keys[...], across, preferred_element_type=jnp.float32),
            lax.dot_general(asked, old_keys[...], across, preferred_element_type=jnp.float32),
        ) / math.sqrt(head)
        exponent = jnp.exp(scores - jnp.max(scores, axis=-1, keepdims=True))
        probs = exponent / jnp.sum(exponent, axis=-1, keepdims=True)
        fresh = jnp.where(seen, probs, 0.0).astype(jnp.bfloat16)
        stale = jnp.where(seen, 0.0, probs).astype(jnp.bfloat16)
        attended[rows, my_head] = (
            jnp.dot(fresh, values[...], preferred_element_type=jnp.float32)
            + jnp.dot(stale, old_values[...], preferred_element_type=jnp.float32)
        ).astype(jnp.bfloat16)
        return carry

    lax.fori_loop(0, CHUNKS, attend, 0)

    def heads(origin):
        return attended.at[:, pl.ds(pl.multiple_of(origin * head, head), head)]

    def a_copy(step):
        place = heads(me)
        return remote(place, place, a_send.at[step], a_recv.at[me], slow_peer(step) * fast + b)

    def a_forward(origin_slow, step):
        origin = origin_slow * fast + b
        place = heads(origin)
        return remote(
            place, place, a_pass.at[origin_slow, step], a_recv.at[origin], a * fast + fast_peer(step)
        )

    def a_arrival(origin):
        place = heads(origin)
        return remote(place, place, a_send.at[0], a_recv.at[origin], other(1))

    for step in range(1, slow):
        a_copy(step).start()
    for hop in range(1, fast):
        a_forward(a, hop).start()

    back = (((0,), (0,)), ((), ()))
    new_keys[...] = lax.dot_general(
        pick[...], keys[...], back, preferred_element_type=jnp.float32
    ).astype(jnp.bfloat16)
    new_values[...] = lax.dot_general(
        pick[...], values[...], back, preferred_element_type=jnp.float32
    ).astype(jnp.bfloat16)

    for step in range(1, slow):
        origin_slow = slow_peer(step)
        a_arrival(origin_slow * fast + b).wait_recv()
        for hop in range(1, fast):
            a_forward(origin_slow, hop).start()
    for step in range(1, members):
        w_arrival(step).wait_recv()
        twin_copy(step, core).start()
    for hop in range(1, fast):
        for step in range(slow):
            a_arrival(slow_peer(step) * fast + fast_peer(hop)).wait_recv()
    for step in range(1, members):
        twin_copy(step, 1 - core).wait_recv()
    my_gate = gate[:, pl.ds(pl.multiple_of(me * part, 128), part)] if aligned else gate[me]

    def s_copy(step, r):
        rows = pl.ds(pl.multiple_of(r * chunk, chunk), chunk)
        return remote(
            updated.at[rows],
            piece(me, r),
            s_send.at[step, r],
            s_recv.at[me, r],
            slow_peer(step) * fast + b,
            section + 1,
        )

    def finish(r, carry):
        rows = pl.ds(pl.multiple_of(r * chunk, chunk), chunk)
        branch = jnp.dot(attended[rows, :], out_cols[...], preferred_element_type=jnp.float32)
        updated[rows, :] = (state[me, rows].astype(jnp.float32) + my_gate * branch).astype(jnp.bfloat16)

        @pl.when(jnp.logical_not(last))
        def _():
            for step in range(slow):
                s_copy(step, r).start()

        return carry

    lax.fori_loop(0, CHUNKS, finish, 0)

    def o_copy(step):
        target = other(step)
        return remote(
            updated.at[pl.ds(pl.multiple_of(target * mine, mine), mine)],
            landed.at[me],
            o_send.at[step],
            o_recv.at[me],
            target,
        )

    def o_arrival(step):
        origin = other(step)
        return remote(landed.at[origin], landed.at[origin], o_send.at[step], o_recv.at[origin], origin)

    for step in range(1, members):
        o_copy(step).start()
    landed[me] = updated[pl.ds(pl.multiple_of(me * mine, mine), mine), :]

    for step in range(1, members):
        w_copy(step).wait_send()
        twin_copy(step, core).wait_send()
    for step in range(1, slow):
        a_copy(step).wait_send()
    for hop in range(1, fast):
        for step in range(slow):
            a_forward(slow_peer(step), hop).wait_send()

    def drain(r, carry):
        @pl.when(jnp.logical_not(last))
        def _():
            for step in range(slow):
                s_copy(step, r).wait_send()

        @pl.when(jnp.logical_not(first))
        def _():
            for step in range(slow):
                for hop in range(1, fast):
                    s_forward(slow_peer(step), hop, r).wait_send()

        return carry

    lax.fori_loop(0, CHUNKS, drain, 0)
    for step in range(1, members):
        o_arrival(step).wait_recv()
    for step in range(1, members):
        o_copy(step).wait_send()
    if aligned:
        for k in range(members):
            result[:, k * part : (k + 1) * part] = landed[k]
    else:
        result[...] = landed[...]


def per_device(
    hidden_in,
    assign,
    order,
    w_qkv,
    w_out,
    mod_shift,
    mod_scale,
    mod_gate,
    q_gain,
    k_gain,
    stale_keys,
    stale_values,
):
    segments = lax.axis_size("segment")
    members = lax.axis_size("ulysses")
    width = hidden_in.shape[1]
    head = q_gain.shape[1]
    tokens = assign.shape[0]
    patches = order.shape[0]
    local = tokens // patches // members
    mine = patches * local
    part = width // members
    fast = 2 if members % 2 == 0 else 1
    slow = members // fast
    aligned = part % 128 == 0

    def blocks(array):
        if aligned:
            return array
        return array.reshape(array.shape[0], members, part).transpose(1, 0, 2)

    vectors = (1, width) if aligned else (members, 1, part)
    shaped = (mine, width) if aligned else (members, mine, part)
    bf16 = jnp.bfloat16
    inside = pl.BlockSpec(memory_space=pltpu.VMEM)
    dma = pltpu.SemaphoreType.DMA
    result, new_keys, new_values = pl.pallas_call(
        functools.partial(kernel, segments, members, patches),
        out_shape=(
            jax.ShapeDtypeStruct(shaped, bf16),
            jax.ShapeDtypeStruct((tokens, head), bf16),
            jax.ShapeDtypeStruct((tokens, head), bf16),
        ),
        in_specs=[pl.BlockSpec(memory_space=pltpu.SMEM)] + [pl.BlockSpec(memory_space=pltpu.HBM)] * 11,
        out_specs=(inside, inside, inside),
        scratch_shapes=[
            pltpu.VMEM((width, 3 * head), bf16),
            pltpu.VMEM((members, tokens, part), bf16),
            pltpu.VMEM((members, tokens, part), bf16),
            pltpu.VMEM((tokens, tokens), bf16),
        ]
        + [pltpu.VMEM((tokens, head), bf16)] * 7
        + [pltpu.VMEM(vectors, jnp.float32)] * 3
        + [pltpu.VMEM((1, head), jnp.float32)] * 2
        + [
            pltpu.VMEM((1, tokens), jnp.int32),
            pltpu.VMEM((tokens, members * head), bf16),
            pltpu.VMEM((members * head, part), bf16),
            pltpu.VMEM((tokens, part), bf16),
            pltpu.VMEM((members, mine, part), bf16),
            dma((9,)),
            dma((3,)),
            dma((members,)),
            dma((members,)),
            dma((members,)),
            dma((members,)),
            dma((members,)),
            dma((slow,)),
            dma((slow, fast)),
            dma((members,)),
            dma((slow, CHUNKS)),
            dma((slow, fast, CHUNKS)),
            dma((members, CHUNKS)),
            dma((members,)),
            dma((members,)),
        ],
        compiler_params=pltpu.CompilerParams(
            collective_id=0, has_side_effects=True, vmem_limit_bytes=60 * 2**20
        ),
        cost_estimate=pl.CostEstimate(
            flops=2 * tokens * width * 4 * head, bytes_accessed=10**7, transcendentals=tokens * tokens
        ),
    )(
        order,
        w_qkv[0].transpose(1, 0, 2),
        blocks(hidden_in),
        blocks(w_out[0]),
        blocks(mod_shift),
        blocks(mod_scale),
        blocks(mod_gate),
        q_gain,
        k_gain,
        assign[None, :],
        stale_keys[0],
        stale_values[0],
    )
    if not aligned:
        result = result.transpose(1, 0, 2)
    block_out = result.reshape(1, patches, local, width)
    return (block_out, new_keys[None], new_values[None])


def solution(mesh):
    placed = (
        P("rep", None),
        P(),
        P(),
        P("segment", None, None, "ulysses"),
        P("segment", "ulysses", None),
        P("segment", None),
        P("segment", None),
        P("segment", None),
        P("segment", None),
        P("segment", None),
        P("segment", "rep", "ulysses"),
        P("segment", "rep", "ulysses"),
    )
    return jax.shard_map(
        per_device,
        mesh=mesh,
        in_specs=placed,
        out_specs=(
            P("segment", "rep", "ulysses", None),
            P("segment", "rep", "ulysses"),
            P("segment", "rep", "ulysses"),
        ),
        check_vma=False,
    )
```

```python
import functools
import math

import jax
import jax.numpy as jnp
from jax import lax
from jax.experimental import pallas as pl
from jax.experimental.pallas import tpu as pltpu
from jax.sharding import PartitionSpec as P

MESH = pl.DeviceIdType.MESH
CHUNKS = 4


def kernel(
    segments,
    members,
    patches,
    order,
    weights_in,
    hidden,
    out_rows,
    shift_in,
    scale_in,
    gate_in,
    q_gain_in,
    k_gain_in,
    assign_in,
    stale_keys_in,
    stale_values_in,
    result,
    new_keys,
    new_values,
    weights,
    raw,
    state,
    pick,
    queries,
    keys,
    values,
    stale_keys,
    stale_values,
    old_keys,
    old_values,
    shift,
    scale,
    gate,
    q_gain,
    k_gain,
    assign,
    attended,
    out_cols,
    updated,
    landed,
    load_sem,
    wide_sem,
    raw_sem,
    w_send,
    w_recv,
    w_pass,
    w_twin,
    a_send,
    a_pass,
    a_recv,
    s_send,
    s_pass,
    s_recv,
    o_send,
    o_recv,
):
    fast = 2 if members % 2 == 0 else 1
    slow = members // fast
    section = lax.axis_index("segment")
    me = lax.axis_index("ulysses")
    core = lax.axis_index("rep")
    a, b = me // fast, lax.rem(me, fast)
    tokens, head = stale_keys.shape
    part = state.shape[2]
    width = members * part
    half = head // 2
    aligned = part % 128 == 0
    mine = tokens // members
    chunk = tokens // CHUNKS
    first = section == 0
    last = section == segments - 1

    def columns(ref, index):
        if not aligned:
            return ref.at[index]
        return ref.at[:, pl.ds(pl.multiple_of(index * part, 128), part)]

    def remote(src, dst, send, recv, member, where=None):
        return pltpu.make_async_remote_copy(
            src_ref=src,
            dst_ref=dst,
            send_sem=send,
            recv_sem=recv,
            device_id={"segment": section if where is None else where, "ulysses": member},
            device_id_type=MESH,
        )

    def other(step):
        return lax.rem(me + step, members)

    def slow_peer(step):
        return lax.rem(a + step, slow)

    def fast_peer(step):
        return lax.rem(b + step, fast)

    my_head = pl.ds(pl.multiple_of(me * head, head), head)
    loads = [
        pltpu.make_async_copy(src, dst, load_sem.at[i])
        for i, (src, dst) in enumerate(
            (
                (assign_in, assign),
                (stale_keys_in, stale_keys),
                (stale_values_in, stale_values),
                (shift_in, shift),
                (scale_in, scale),
                (q_gain_in, q_gain),
                (k_gain_in, k_gain),
                (gate_in, gate),
                (columns(out_rows, me), out_cols.at[my_head]),
            )
        )
    ]

    wide_loads = [
        pltpu.make_async_copy(
            weights_in.at[j], weights.at[:, pl.ds(j * head, head)], wide_sem.at[j]
        )
        for j in range(3)
    ]

    def load_raw(k):
        return pltpu.make_async_copy(columns(hidden, k), raw.at[k], raw_sem.at[k])

    for copy in loads:
        copy.start()

    @pl.when(first)
    def _():
        for k in range(members):
            load_raw(k).start()

    for copy in wide_loads:
        copy.start()

    barrier = pltpu.get_barrier_semaphore()

    def greet(member, where):
        pl.semaphore_signal(
            barrier,
            inc=1,
            device_id={"segment": where, "ulysses": member},
            device_id_type=MESH,
        )

    for step in range(1, members):
        greet(other(step), section)

    @pl.when(jnp.logical_not(last))
    def _():
        for step in range(slow):
            greet(slow_peer(step) * fast + b, section + 1)

    @pl.when(jnp.logical_not(first))
    def _():
        for step in range(slow):
            greet(slow_peer(step) * fast + b, section - 1)

    pl.semaphore_signal(
        barrier, inc=1, device_id={"rep": 1 - core}, device_id_type=MESH
    )
    sides = jnp.where(first, 0, 1) + jnp.where(last, 0, 1)
    pl.semaphore_wait(barrier, members + slow * sides)

    def w_place(origin, which):
        return out_cols.at[pl.ds(pl.multiple_of(origin * head + which * half, half), half)]

    def w_copy(step):
        target = other(step)
        rows = pl.ds(pl.multiple_of(core * half, half), half)
        if aligned:
            piece = out_rows.at[rows, pl.ds(pl.multiple_of(target * part, 128), part)]
        else:
            piece = out_rows.at[target, rows]
        return remote(piece, w_place(me, core), w_send.at[step], w_recv.at[me], target)

    def w_arrival(step):
        origin = other(step)
        place = w_place(origin, core)
        return remote(place, place, w_send.at[step], w_recv.at[origin], origin)

    def twin_copy(step, which):
        origin = other(step)
        place = w_place(origin, which)
        return pltpu.make_async_remote_copy(
            src_ref=place,
            dst_ref=place,
            send_sem=w_pass.at[step],
            recv_sem=w_twin.at[origin],
            device_id={"rep": 1 - core},
            device_id_type=MESH,
        )

    for step in range(1, members):
        w_copy(step).start()

    mine_rows = tokens // members
    local = mine_rows // patches

    def turns(index):
        patch = lax.rem(index // local, patches)
        total = jnp.zeros_like(index)
        for i in range(patches):
            total += jnp.where(patch == order[i], i, 0)
        return total

    lane = lax.broadcasted_iota(jnp.int32, (tokens, tokens), 1)
    row = lax.broadcasted_iota(jnp.int32, (tokens, 1), 0)
    source = lax.rem(row // local, patches) * (tokens // patches) + row // mine_rows * local + lax.rem(row, local)
    for copy in loads[:1]:
        copy.wait()
    chosen = jnp.sum(jnp.where(lane == source, assign[...].astype(jnp.float32), 0.0), axis=1, keepdims=True)
    pick[...] = (lane.astype(jnp.float32) == chosen).astype(jnp.float32).astype(jnp.bfloat16)
    for copy in loads[1:]:
        copy.wait()

    def exact(mask, data):
        return jnp.dot(mask, data, preferred_element_type=jnp.float32).astype(jnp.bfloat16)

    old_keys[...] = exact(pick[...], stale_keys[...])
    old_values[...] = exact(pick[...], stale_values[...])

    def piece(origin, r):
        return state.at[origin, pl.ds(pl.multiple_of(r * chunk, chunk), chunk)]

    def s_arrival(origin, r):
        place = piece(origin, r)
        return remote(place, place, s_send.at[0, r], s_recv.at[origin, r], other(1))

    def s_forward(origin_slow, step, r):
        origin = origin_slow * fast + b
        place = piece(origin, r)
        return remote(
            place,
            place,
            s_pass.at[origin_slow, step, r],
            s_recv.at[origin, r],
            a * fast + fast_peer(step),
        )

    @pl.when(first)
    def _():
        for k in range(members):
            load_raw(k).wait()

    for copy in wide_loads:
        copy.wait()

    def gain(data, factor):
        square = jnp.mean(data * data, axis=-1, keepdims=True)
        return (data * lax.rsqrt(square + 1e-06) * factor).astype(jnp.bfloat16)

    def vector(ref, k):
        return ref[:, k * part : (k + 1) * part] if aligned else ref[k]

    def project(r, carry):
        @pl.when(jnp.logical_not(first))
        def _():
            for step in range(slow):
                origin_slow = slow_peer(step)
                s_arrival(origin_slow * fast + b, r).wait_recv()
                for hop in range(1, fast):
                    s_forward(origin_slow, hop, r).start()
            for hop in range(1, fast):
                for step in range(slow):
                    s_arrival(slow_peer(step) * fast + fast_peer(hop), r).wait_recv()

        rows = pl.ds(pl.multiple_of(r * chunk, chunk), chunk)

        @pl.when(first)
        def _():
            for k in range(members):
                state[k, rows] = exact(pick[rows, :], raw[k])

        total = jnp.zeros((chunk, 1), jnp.float32)
        for k in range(members):
            total += jnp.sum(state[k, rows].astype(jnp.float32), axis=-1, keepdims=True)
        mean = total / width
        total = jnp.zeros((chunk, 1), jnp.float32)
        for k in range(members):
            center = state[k, rows].astype(jnp.float32) - mean
            total += jnp.sum(center * center, axis=-1, keepdims=True)
        inverse = lax.rsqrt(total / width + 1e-06)
        projected = jnp.zeros((chunk, 3 * head), jnp.float32)
        for k in range(members):
            center = state[k, rows].astype(jnp.float32) - mean
            normed = (center * inverse * (1.0 + vector(scale, k)) + vector(shift, k)).astype(jnp.bfloat16)
            projected += jnp.dot(
                normed, weights[k * part : (k + 1) * part, :], preferred_element_type=jnp.float32
            )
        queries[rows, :] = gain(projected[:, :head], q_gain[...])
        keys[rows, :] = gain(projected[:, head : 2 * head], k_gain[...])
        values[rows, :] = projected[:, 2 * head :].astype(jnp.bfloat16)
        return carry

    lax.fori_loop(0, CHUNKS, project, 0)

    def heads(origin, r):
        return attended.at[
            pl.ds(pl.multiple_of(r * chunk, chunk), chunk),
            pl.ds(pl.multiple_of(origin * head, head), head),
        ]

    def a_copy(step, r):
        place = heads(me, r)
        return remote(place, place, a_send.at[step, r], a_recv.at[me, r], slow_peer(step) * fast + b)

    def a_forward(origin_slow, step, r):
        origin = origin_slow * fast + b
        place = heads(origin, r)
        return remote(
            place, place, a_pass.at[origin_slow, step, r], a_recv.at[origin, r], a * fast + fast_peer(step)
        )

    def a_arrival(origin, r):
        place = heads(origin, r)
        return remote(place, place, a_send.at[0, r], a_recv.at[origin, r], other(1))

    def attend(r, carry):
        rows = pl.ds(pl.multiple_of(r * chunk, chunk), chunk)
        asking = lax.broadcasted_iota(jnp.int32, (chunk, tokens), 0) + r * chunk
        asked_of = lax.broadcasted_iota(jnp.int32, (chunk, tokens), 1)
        seen = turns(asked_of) <= turns(asking)
        across = (((1,), (1,)), ((), ()))
        asked = queries[rows, :]
        scores = jnp.where(
            seen,
            lax.dot_general(asked, keys[...], across, preferred_element_type=jnp.float32),
            lax.dot_general(asked, old_keys[...], across, preferred_element_type=jnp.float32),
        ) / math.sqrt(head)
        exponent = jnp.exp(scores - jnp.max(scores, axis=-1, keepdims=True))
        probs = exponent / jnp.sum(exponent, axis=-1, keepdims=True)
        fresh = jnp.where(seen, probs, 0.0).astype(jnp.bfloat16)
        stale = jnp.where(seen, 0.0, probs).astype(jnp.bfloat16)
        attended[rows, my_head] = (
            jnp.dot(fresh, values[...], preferred_element_type=jnp.float32)
            + jnp.dot(stale, old_values[...], preferred_element_type=jnp.float32)
        ).astype(jnp.bfloat16)
        for step in range(1, slow):
            a_copy(step, r).start()
        for hop in range(1, fast):
            a_forward(a, hop, r).start()
        return carry

    lax.fori_loop(0, CHUNKS, attend, 0)

    back = (((0,), (0,)), ((), ()))
    new_keys[...] = lax.dot_general(
        pick[...], keys[...], back, preferred_element_type=jnp.float32
    ).astype(jnp.bfloat16)
    new_values[...] = lax.dot_general(
        pick[...], values[...], back, preferred_element_type=jnp.float32
    ).astype(jnp.bfloat16)

    def pass_on(r):
        for step in range(1, slow):
            origin_slow = slow_peer(step)
            a_arrival(origin_slow * fast + b, r).wait_recv()
            for hop in range(1, fast):
                a_forward(origin_slow, hop, r).start()

    for step in range(1, members):
        w_arrival(step).wait_recv()
        twin_copy(step, core).start()
    pass_on(0)
    for step in range(1, members):
        twin_copy(step, 1 - core).wait_recv()
    my_gate = gate[:, pl.ds(pl.multiple_of(me * part, 128), part)] if aligned else gate[me]

    def s_copy(step, r):
        rows = pl.ds(pl.multiple_of(r * chunk, chunk), chunk)
        return remote(
            updated.at[rows],
            piece(me, r),
            s_send.at[step, r],
            s_recv.at[me, r],
            slow_peer(step) * fast + b,
            section + 1,
        )

    def o_copy(target):
        return remote(
            updated.at[pl.ds(pl.multiple_of(target * mine, mine), mine)],
            landed.at[me],
            o_send.at[target],
            o_recv.at[me],
            target,
        )

    def o_arrival(step):
        origin = other(step)
        return remote(landed.at[origin], landed.at[origin], o_send.at[origin], o_recv.at[origin], origin)

    def o_start(r):
        for i in range(members // CHUNKS):
            target = r * (members // CHUNKS) + i

            @pl.when(target != me)
            def _():
                o_copy(target).start()

    def finish(r, carry):
        @pl.when(r + 1 < CHUNKS)
        def _():
            pass_on(r + 1)

        for hop in range(1, fast):
            for step in range(slow):
                a_arrival(slow_peer(step) * fast + fast_peer(hop), r).wait_recv()
        rows = pl.ds(pl.multiple_of(r * chunk, chunk), chunk)
        branch = jnp.dot(attended[rows, :], out_cols[...], preferred_element_type=jnp.float32)
        updated[rows, :] = (state[me, rows].astype(jnp.float32) + my_gate * branch).astype(jnp.bfloat16)

        @pl.when(jnp.logical_not(last))
        def _():
            for step in range(slow):
                s_copy(step, r).start()

        @pl.when(last)
        def _():
            o_start(r)

        return carry

    lax.fori_loop(0, CHUNKS, finish, 0)

    @pl.when(jnp.logical_not(last))
    def _():
        for r in range(CHUNKS):
            o_start(r)

    landed[me] = updated[pl.ds(pl.multiple_of(me * mine, mine), mine), :]

    for step in range(1, members):
        w_copy(step).wait_send()
        twin_copy(step, core).wait_send()
    def drain(r, carry):
        for step in range(1, slow):
            a_copy(step, r).wait_send()
        for hop in range(1, fast):
            for step in range(slow):
                a_forward(slow_peer(step), hop, r).wait_send()

        @pl.when(jnp.logical_not(last))
        def _():
            for step in range(slow):
                s_copy(step, r).wait_send()

        @pl.when(jnp.logical_not(first))
        def _():
            for step in range(slow):
                for hop in range(1, fast):
                    s_forward(slow_peer(step), hop, r).wait_send()

        return carry

    lax.fori_loop(0, CHUNKS, drain, 0)
    for step in range(1, members):
        o_arrival(step).wait_recv()
    for step in range(1, members):
        o_copy(other(step)).wait_send()
    if aligned:
        for k in range(members):
            result[:, k * part : (k + 1) * part] = landed[k]
    else:
        result[...] = landed[...]


def per_device(
    hidden_in,
    assign,
    order,
    w_qkv,
    w_out,
    mod_shift,
    mod_scale,
    mod_gate,
    q_gain,
    k_gain,
    stale_keys,
    stale_values,
):
    segments = lax.axis_size("segment")
    members = lax.axis_size("ulysses")
    width = hidden_in.shape[1]
    head = q_gain.shape[1]
    tokens = assign.shape[0]
    patches = order.shape[0]
    local = tokens // patches // members
    mine = patches * local
    part = width // members
    fast = 2 if members % 2 == 0 else 1
    slow = members // fast
    aligned = part % 128 == 0

    def blocks(array):
        if aligned:
            return array
        return array.reshape(array.shape[0], members, part).transpose(1, 0, 2)

    vectors = (1, width) if aligned else (members, 1, part)
    shaped = (mine, width) if aligned else (members, mine, part)
    bf16 = jnp.bfloat16
    inside = pl.BlockSpec(memory_space=pltpu.VMEM)
    dma = pltpu.SemaphoreType.DMA
    result, new_keys, new_values = pl.pallas_call(
        functools.partial(kernel, segments, members, patches),
        out_shape=(
            jax.ShapeDtypeStruct(shaped, bf16),
            jax.ShapeDtypeStruct((tokens, head), bf16),
            jax.ShapeDtypeStruct((tokens, head), bf16),
        ),
        in_specs=[pl.BlockSpec(memory_space=pltpu.SMEM)] + [pl.BlockSpec(memory_space=pltpu.HBM)] * 11,
        out_specs=(inside, inside, inside),
        scratch_shapes=[
            pltpu.VMEM((width, 3 * head), bf16),
            pltpu.VMEM((members, tokens, part), bf16),
            pltpu.VMEM((members, tokens, part), bf16),
            pltpu.VMEM((tokens, tokens), bf16),
        ]
        + [pltpu.VMEM((tokens, head), bf16)] * 7
        + [pltpu.VMEM(vectors, jnp.float32)] * 3
        + [pltpu.VMEM((1, head), jnp.float32)] * 2
        + [
            pltpu.VMEM((1, tokens), jnp.int32),
            pltpu.VMEM((tokens, members * head), bf16),
            pltpu.VMEM((members * head, part), bf16),
            pltpu.VMEM((tokens, part), bf16),
            pltpu.VMEM((members, mine, part), bf16),
            dma((9,)),
            dma((3,)),
            dma((members,)),
            dma((members,)),
            dma((members,)),
            dma((members,)),
            dma((members,)),
            dma((slow, CHUNKS)),
            dma((slow, fast, CHUNKS)),
            dma((members, CHUNKS)),
            dma((slow, CHUNKS)),
            dma((slow, fast, CHUNKS)),
            dma((members, CHUNKS)),
            dma((members,)),
            dma((members,)),
        ],
        compiler_params=pltpu.CompilerParams(
            collective_id=0, has_side_effects=True, vmem_limit_bytes=60 * 2**20
        ),
        cost_estimate=pl.CostEstimate(
            flops=2 * tokens * width * 4 * head, bytes_accessed=10**7, transcendentals=tokens * tokens
        ),
    )(
        order,
        w_qkv[0].transpose(1, 0, 2),
        blocks(hidden_in),
        blocks(w_out[0]),
        blocks(mod_shift),
        blocks(mod_scale),
        blocks(mod_gate),
        q_gain,
        k_gain,
        assign[None, :],
        stale_keys[0],
        stale_values[0],
    )
    if not aligned:
        result = result.transpose(1, 0, 2)
    block_out = result.reshape(1, patches, local, width)
    return (block_out, new_keys[None], new_values[None])


def solution(mesh):
    placed = (
        P("rep", None),
        P(),
        P(),
        P("segment", None, None, "ulysses"),
        P("segment", "ulysses", None),
        P("segment", None),
        P("segment", None),
        P("segment", None),
        P("segment", None),
        P("segment", None),
        P("segment", "rep", "ulysses"),
        P("segment", "rep", "ulysses"),
    )
    return jax.shard_map(
        per_device,
        mesh=mesh,
        in_specs=placed,
        out_specs=(
            P("segment", "rep", "ulysses", None),
            P("segment", "rep", "ulysses"),
            P("segment", "rep", "ulysses"),
        ),
        check_vma=False,
    )
```

```python
import functools
import math

import jax
import jax.numpy as jnp
from jax import lax
from jax.experimental import pallas as pl
from jax.experimental.pallas import tpu as pltpu
from jax.sharding import PartitionSpec as P

MESH = pl.DeviceIdType.MESH
CHUNKS = 4


def kernel(
    segments,
    members,
    patches,
    order,
    weights_in,
    hidden,
    out_rows,
    shift_in,
    scale_in,
    gate_in,
    q_gain_in,
    k_gain_in,
    assign_in,
    stale_keys_in,
    stale_values_in,
    result,
    new_keys,
    new_values,
    weights,
    raw,
    state,
    pick,
    queries,
    keys,
    values,
    stale_keys,
    stale_values,
    old_keys,
    old_values,
    shift,
    scale,
    gate,
    q_gain,
    k_gain,
    assign,
    attended,
    out_cols,
    updated,
    landed,
    load_sem,
    wide_sem,
    raw_sem,
    w_send,
    w_recv,
    w_pass,
    w_twin,
    a_send,
    a_pass,
    a_recv,
    s_send,
    s_pass,
    s_recv,
    o_send,
    o_recv,
):
    fast = 2 if members % 2 == 0 else 1
    slow = members // fast
    section = lax.axis_index("segment")
    me = lax.axis_index("ulysses")
    core = lax.axis_index("rep")
    a, b = me // fast, lax.rem(me, fast)
    tokens, head = stale_keys.shape
    part = state.shape[2]
    width = members * part
    half = head // 2
    aligned = part % 128 == 0
    mine = tokens // members
    chunk = tokens // CHUNKS
    first = section == 0
    last = section == segments - 1

    def columns(ref, index):
        if not aligned:
            return ref.at[index]
        return ref.at[:, pl.ds(pl.multiple_of(index * part, 128), part)]

    def remote(src, dst, send, recv, member, where=None):
        return pltpu.make_async_remote_copy(
            src_ref=src,
            dst_ref=dst,
            send_sem=send,
            recv_sem=recv,
            device_id={"segment": section if where is None else where, "ulysses": member},
            device_id_type=MESH,
        )

    def other(step):
        return lax.rem(me + step, members)

    def slow_peer(step):
        return lax.rem(a + step, slow)

    def fast_peer(step):
        return lax.rem(b + step, fast)

    my_head = pl.ds(pl.multiple_of(me * head, head), head)
    loads = [
        pltpu.make_async_copy(src, dst, load_sem.at[i])
        for i, (src, dst) in enumerate(
            (
                (assign_in, assign),
                (stale_keys_in, stale_keys),
                (stale_values_in, stale_values),
                (shift_in, shift),
                (scale_in, scale),
                (q_gain_in, q_gain),
                (k_gain_in, k_gain),
                (gate_in, gate),
                (columns(out_rows, me), out_cols.at[my_head]),
            )
        )
    ]

    wide_loads = [
        pltpu.make_async_copy(
            weights_in.at[j], weights.at[:, pl.ds(j * head, head)], wide_sem.at[j]
        )
        for j in range(3)
    ]

    def load_raw(k):
        return pltpu.make_async_copy(columns(hidden, k), raw.at[k], raw_sem.at[k])

    for copy in loads:
        copy.start()

    @pl.when(first)
    def _():
        for k in range(members):
            load_raw(k).start()

    for copy in wide_loads:
        copy.start()

    barrier = pltpu.get_barrier_semaphore()

    def greet(member, where):
        pl.semaphore_signal(
            barrier,
            inc=1,
            device_id={"segment": where, "ulysses": member},
            device_id_type=MESH,
        )

    for step in range(1, members):
        greet(other(step), section)

    @pl.when(jnp.logical_not(last))
    def _():
        for step in range(slow):
            greet(slow_peer(step) * fast + b, section + 1)

    @pl.when(jnp.logical_not(first))
    def _():
        for step in range(slow):
            greet(slow_peer(step) * fast + b, section - 1)

    pl.semaphore_signal(
        barrier, inc=1, device_id={"rep": 1 - core}, device_id_type=MESH
    )
    sides = jnp.where(first, 0, 1) + jnp.where(last, 0, 1)
    pl.semaphore_wait(barrier, members + slow * sides)

    def w_place(origin, which):
        return out_cols.at[pl.ds(pl.multiple_of(origin * head + which * half, half), half)]

    def w_copy(step):
        target = other(step)
        rows = pl.ds(pl.multiple_of(core * half, half), half)
        if aligned:
            piece = out_rows.at[rows, pl.ds(pl.multiple_of(target * part, 128), part)]
        else:
            piece = out_rows.at[target, rows]
        return remote(piece, w_place(me, core), w_send.at[step], w_recv.at[me], target)

    def w_arrival(step):
        origin = other(step)
        place = w_place(origin, core)
        return remote(place, place, w_send.at[step], w_recv.at[origin], origin)

    def twin_copy(step, which):
        origin = other(step)
        place = w_place(origin, which)
        return pltpu.make_async_remote_copy(
            src_ref=place,
            dst_ref=place,
            send_sem=w_pass.at[step],
            recv_sem=w_twin.at[origin],
            device_id={"rep": 1 - core},
            device_id_type=MESH,
        )

    for step in range(1, members):
        w_copy(step).start()

    mine_rows = tokens // members
    local = mine_rows // patches

    def turns(index):
        patch = lax.rem(index // local, patches)
        total = jnp.zeros_like(index)
        for i in range(patches):
            total += jnp.where(patch == order[i], i, 0)
        return total

    lane = lax.broadcasted_iota(jnp.int32, (tokens, tokens), 1)
    row = lax.broadcasted_iota(jnp.int32, (tokens, 1), 0)
    source = lax.rem(row // local, patches) * (tokens // patches) + row // mine_rows * local + lax.rem(row, local)
    for copy in loads[:1]:
        copy.wait()
    chosen = jnp.sum(jnp.where(lane == source, assign[...].astype(jnp.float32), 0.0), axis=1, keepdims=True)
    pick[...] = (lane.astype(jnp.float32) == chosen).astype(jnp.float32).astype(jnp.bfloat16)
    for copy in loads[1:]:
        copy.wait()

    def exact(mask, data):
        return jnp.dot(mask, data, preferred_element_type=jnp.float32).astype(jnp.bfloat16)

    old_keys[...] = exact(pick[...], stale_keys[...])
    old_values[...] = exact(pick[...], stale_values[...])

    def piece(origin, r):
        return state.at[origin, pl.ds(pl.multiple_of(r * chunk, chunk), chunk)]

    def s_arrival(origin, r):
        place = piece(origin, r)
        return remote(place, place, s_send.at[0, r], s_recv.at[origin, r], other(1))

    def s_forward(origin_slow, step, r):
        origin = origin_slow * fast + b
        place = piece(origin, r)
        return remote(
            place,
            place,
            s_pass.at[origin_slow, step, r],
            s_recv.at[origin, r],
            a * fast + fast_peer(step),
        )

    @pl.when(first)
    def _():
        for k in range(members):
            load_raw(k).wait()

    for copy in wide_loads:
        copy.wait()

    def gain(data, factor):
        square = jnp.mean(data * data, axis=-1, keepdims=True)
        return (data * lax.rsqrt(square + 1e-06) * factor).astype(jnp.bfloat16)

    def vector(ref, k):
        return ref[:, k * part : (k + 1) * part] if aligned else ref[k]

    def pass_state(r):
        for step in range(slow):
            origin_slow = slow_peer(step)
            s_arrival(origin_slow * fast + b, r).wait_recv()
            for hop in range(1, fast):
                s_forward(origin_slow, hop, r).start()

    @pl.when(jnp.logical_not(first))
    def _():
        pass_state(0)

    def project(r, carry):
        @pl.when(jnp.logical_and(jnp.logical_not(first), r + 1 < CHUNKS))
        def _():
            pass_state(r + 1)

        @pl.when(jnp.logical_not(first))
        def _():
            for hop in range(1, fast):
                for step in range(slow):
                    s_arrival(slow_peer(step) * fast + fast_peer(hop), r).wait_recv()

        rows = pl.ds(pl.multiple_of(r * chunk, chunk), chunk)

        @pl.when(first)
        def _():
            for k in range(members):
                state[k, rows] = exact(pick[rows, :], raw[k])

        total = jnp.zeros((chunk, 1), jnp.float32)
        for k in range(members):
            total += jnp.sum(state[k, rows].astype(jnp.float32), axis=-1, keepdims=True)
        mean = total / width
        total = jnp.zeros((chunk, 1), jnp.float32)
        for k in range(members):
            center = state[k, rows].astype(jnp.float32) - mean
            total += jnp.sum(center * center, axis=-1, keepdims=True)
        inverse = lax.rsqrt(total / width + 1e-06)
        projected = jnp.zeros((chunk, 3 * head), jnp.float32)
        for k in range(members):
            center = state[k, rows].astype(jnp.float32) - mean
            normed = (center * inverse * (1.0 + vector(scale, k)) + vector(shift, k)).astype(jnp.bfloat16)
            projected += jnp.dot(
                normed, weights[k * part : (k + 1) * part, :], preferred_element_type=jnp.float32
            )
        queries[rows, :] = gain(projected[:, :head], q_gain[...])
        keys[rows, :] = gain(projected[:, head : 2 * head], k_gain[...])
        values[rows, :] = projected[:, 2 * head :].astype(jnp.bfloat16)
        return carry

    lax.fori_loop(0, CHUNKS, project, 0)

    def heads(origin, r):
        return attended.at[
            pl.ds(pl.multiple_of(r * chunk, chunk), chunk),
            pl.ds(pl.multiple_of(origin * head, head), head),
        ]

    def a_copy(step, r):
        place = heads(me, r)
        return remote(place, place, a_send.at[step, r], a_recv.at[me, r], slow_peer(step) * fast + b)

    def a_forward(origin_slow, step, r):
        origin = origin_slow * fast + b
        place = heads(origin, r)
        return remote(
            place, place, a_pass.at[origin_slow, step, r], a_recv.at[origin, r], a * fast + fast_peer(step)
        )

    def a_arrival(origin, r):
        place = heads(origin, r)
        return remote(place, place, a_send.at[0, r], a_recv.at[origin, r], other(1))

    def attend(r, carry):
        rows = pl.ds(pl.multiple_of(r * chunk, chunk), chunk)
        asking = lax.broadcasted_iota(jnp.int32, (chunk, tokens), 0) + r * chunk
        asked_of = lax.broadcasted_iota(jnp.int32, (chunk, tokens), 1)
        seen = turns(asked_of) <= turns(asking)
        across = (((1,), (1,)), ((), ()))
        asked = queries[rows, :]
        scores = jnp.where(
            seen,
            lax.dot_general(asked, keys[...], across, preferred_element_type=jnp.float32),
            lax.dot_general(asked, old_keys[...], across, preferred_element_type=jnp.float32),
        ) / math.sqrt(head)
        exponent = jnp.exp(scores - jnp.max(scores, axis=-1, keepdims=True))
        probs = exponent / jnp.sum(exponent, axis=-1, keepdims=True)
        fresh = jnp.where(seen, probs, 0.0).astype(jnp.bfloat16)
        stale = jnp.where(seen, 0.0, probs).astype(jnp.bfloat16)
        attended[rows, my_head] = (
            jnp.dot(fresh, values[...], preferred_element_type=jnp.float32)
            + jnp.dot(stale, old_values[...], preferred_element_type=jnp.float32)
        ).astype(jnp.bfloat16)
        for step in range(1, slow):
            a_copy(step, r).start()
        for hop in range(1, fast):
            a_forward(a, hop, r).start()
        return carry

    lax.fori_loop(0, CHUNKS, attend, 0)

    back = (((0,), (0,)), ((), ()))
    new_keys[...] = lax.dot_general(
        pick[...], keys[...], back, preferred_element_type=jnp.float32
    ).astype(jnp.bfloat16)
    new_values[...] = lax.dot_general(
        pick[...], values[...], back, preferred_element_type=jnp.float32
    ).astype(jnp.bfloat16)

    def pass_on(r):
        for step in range(1, slow):
            origin_slow = slow_peer(step)
            a_arrival(origin_slow * fast + b, r).wait_recv()
            for hop in range(1, fast):
                a_forward(origin_slow, hop, r).start()

    for step in range(1, members):
        w_arrival(step).wait_recv()
        twin_copy(step, core).start()
    pass_on(0)
    for step in range(1, members):
        twin_copy(step, 1 - core).wait_recv()
    my_gate = gate[:, pl.ds(pl.multiple_of(me * part, 128), part)] if aligned else gate[me]

    def s_copy(step, r):
        rows = pl.ds(pl.multiple_of(r * chunk, chunk), chunk)
        return remote(
            updated.at[rows],
            piece(me, r),
            s_send.at[step, r],
            s_recv.at[me, r],
            slow_peer(step) * fast + b,
            section + 1,
        )

    def o_copy(target):
        return remote(
            updated.at[pl.ds(pl.multiple_of(target * mine, mine), mine)],
            landed.at[me],
            o_send.at[target],
            o_recv.at[me],
            target,
        )

    def o_arrival(step):
        origin = other(step)
        return remote(landed.at[origin], landed.at[origin], o_send.at[origin], o_recv.at[origin], origin)

    def o_start(r):
        for i in range(members // CHUNKS):
            target = r * (members // CHUNKS) + i

            @pl.when(target != me)
            def _():
                o_copy(target).start()

    def finish(r, carry):
        @pl.when(r + 1 < CHUNKS)
        def _():
            pass_on(r + 1)

        for hop in range(1, fast):
            for step in range(slow):
                a_arrival(slow_peer(step) * fast + fast_peer(hop), r).wait_recv()
        rows = pl.ds(pl.multiple_of(r * chunk, chunk), chunk)
        branch = jnp.dot(attended[rows, :], out_cols[...], preferred_element_type=jnp.float32)
        updated[rows, :] = (state[me, rows].astype(jnp.float32) + my_gate * branch).astype(jnp.bfloat16)

        @pl.when(jnp.logical_not(last))
        def _():
            for step in range(slow):
                s_copy(step, r).start()

        @pl.when(last)
        def _():
            o_start(r)

        return carry

    lax.fori_loop(0, CHUNKS, finish, 0)

    @pl.when(jnp.logical_not(last))
    def _():
        for r in range(CHUNKS):
            o_start(r)

    landed[me] = updated[pl.ds(pl.multiple_of(me * mine, mine), mine), :]

    for step in range(1, members):
        w_copy(step).wait_send()
        twin_copy(step, core).wait_send()
    def drain(r, carry):
        for step in range(1, slow):
            a_copy(step, r).wait_send()
        for hop in range(1, fast):
            for step in range(slow):
                a_forward(slow_peer(step), hop, r).wait_send()

        @pl.when(jnp.logical_not(last))
        def _():
            for step in range(slow):
                s_copy(step, r).wait_send()

        @pl.when(jnp.logical_not(first))
        def _():
            for step in range(slow):
                for hop in range(1, fast):
                    s_forward(slow_peer(step), hop, r).wait_send()

        return carry

    lax.fori_loop(0, CHUNKS, drain, 0)
    for step in range(1, members):
        o_arrival(step).wait_recv()
    for step in range(1, members):
        o_copy(other(step)).wait_send()
    if aligned:
        for k in range(members):
            result[:, k * part : (k + 1) * part] = landed[k]
    else:
        result[...] = landed[...]


def per_device(
    hidden_in,
    assign,
    order,
    w_qkv,
    w_out,
    mod_shift,
    mod_scale,
    mod_gate,
    q_gain,
    k_gain,
    stale_keys,
    stale_values,
):
    segments = lax.axis_size("segment")
    members = lax.axis_size("ulysses")
    width = hidden_in.shape[1]
    head = q_gain.shape[1]
    tokens = assign.shape[0]
    patches = order.shape[0]
    local = tokens // patches // members
    mine = patches * local
    part = width // members
    fast = 2 if members % 2 == 0 else 1
    slow = members // fast
    aligned = part % 128 == 0

    def blocks(array):
        if aligned:
            return array
        return array.reshape(array.shape[0], members, part).transpose(1, 0, 2)

    vectors = (1, width) if aligned else (members, 1, part)
    shaped = (mine, width) if aligned else (members, mine, part)
    bf16 = jnp.bfloat16
    inside = pl.BlockSpec(memory_space=pltpu.VMEM)
    dma = pltpu.SemaphoreType.DMA
    result, new_keys, new_values = pl.pallas_call(
        functools.partial(kernel, segments, members, patches),
        out_shape=(
            jax.ShapeDtypeStruct(shaped, bf16),
            jax.ShapeDtypeStruct((tokens, head), bf16),
            jax.ShapeDtypeStruct((tokens, head), bf16),
        ),
        in_specs=[pl.BlockSpec(memory_space=pltpu.SMEM)] + [pl.BlockSpec(memory_space=pltpu.HBM)] * 11,
        out_specs=(inside, inside, inside),
        scratch_shapes=[
            pltpu.VMEM((width, 3 * head), bf16),
            pltpu.VMEM((members, tokens, part), bf16),
            pltpu.VMEM((members, tokens, part), bf16),
            pltpu.VMEM((tokens, tokens), bf16),
        ]
        + [pltpu.VMEM((tokens, head), bf16)] * 7
        + [pltpu.VMEM(vectors, jnp.float32)] * 3
        + [pltpu.VMEM((1, head), jnp.float32)] * 2
        + [
            pltpu.VMEM((1, tokens), jnp.int32),
            pltpu.VMEM((tokens, members * head), bf16),
            pltpu.VMEM((members * head, part), bf16),
            pltpu.VMEM((tokens, part), bf16),
            pltpu.VMEM((members, mine, part), bf16),
            dma((9,)),
            dma((3,)),
            dma((members,)),
            dma((members,)),
            dma((members,)),
            dma((members,)),
            dma((members,)),
            dma((slow, CHUNKS)),
            dma((slow, fast, CHUNKS)),
            dma((members, CHUNKS)),
            dma((slow, CHUNKS)),
            dma((slow, fast, CHUNKS)),
            dma((members, CHUNKS)),
            dma((members,)),
            dma((members,)),
        ],
        compiler_params=pltpu.CompilerParams(
            collective_id=0, has_side_effects=True, vmem_limit_bytes=60 * 2**20
        ),
        cost_estimate=pl.CostEstimate(
            flops=2 * tokens * width * 4 * head, bytes_accessed=10**7, transcendentals=tokens * tokens
        ),
    )(
        order,
        w_qkv[0].transpose(1, 0, 2),
        blocks(hidden_in),
        blocks(w_out[0]),
        blocks(mod_shift),
        blocks(mod_scale),
        blocks(mod_gate),
        q_gain,
        k_gain,
        assign[None, :],
        stale_keys[0],
        stale_values[0],
    )
    if not aligned:
        result = result.transpose(1, 0, 2)
    block_out = result.reshape(1, patches, local, width)
    return (block_out, new_keys[None], new_values[None])


def solution(mesh):
    placed = (
        P("rep", None),
        P(),
        P(),
        P("segment", None, None, "ulysses"),
        P("segment", "ulysses", None),
        P("segment", None),
        P("segment", None),
        P("segment", None),
        P("segment", None),
        P("segment", None),
        P("segment", "rep", "ulysses"),
        P("segment", "rep", "ulysses"),
    )
    return jax.shard_map(
        per_device,
        mesh=mesh,
        in_specs=placed,
        out_specs=(
            P("segment", "rep", "ulysses", None),
            P("segment", "rep", "ulysses"),
            P("segment", "rep", "ulysses"),
        ),
        check_vma=False,
    )
```
